256 devices in a mesh: batch: 32 (over z, y_hi, core), slab: 8 (over x, y_lo).
Axes of the slice: x: 4, y: 4 (y_hi: 2, y_lo: 2; y = y_hi * 2 + y_lo), z: 8, core: 2. Of those that a mesh axis runs over, the one named last changes fastest.
Arguments:
- lambda_pairs: bfloat16 [64, 800, 800], P('batch', 'slab'), may hold values from -6 to 6
- vvvo: bfloat16 [768, 800, 800], P('batch', 'slab'), may hold values from -0.21875 to 0.21875
- pair_list: int32 [64, 2], P('batch'), may hold values from 0 to 99
- owned_occ: int32 [32], replicated, may hold values from 0 to 99, as said below
- step_root: int32 [2], replicated, may hold values from 0 to 31
- occ_energy: float32 [100], replicated, may hold values from -30 to -0.2
- virt_energy: float32 [800], replicated, may hold values from 0.02 to 40
Outputs:
- residual: float32 [64, 800, 800], P('batch', 'slab')
The draws below stay inside these ranges and needn't reach their ends.
Inputs may be any that keep to these rules, and one draw needn't show every extreme that they name: `owned_occ`: the 32 entries are distinct occupied indices, and 0 and 99 are always among them.
All inputs are finite; a program needn't handle non-finite values.
Results may differ from the reference program's by a relative error of at most 0.00066.
Values may be sent and summed in bfloat16 or wider, within the bound.
No kernel may reach another device: no remote copies, remote signals or barrier semaphores. Data moves between devices by JAX's collectives and lax.ppermute only.
A program may use at most 128 MiB of HBM per device.

```python
import jax
import jax.numpy as jnp
from jax import lax

NO = 100
NV = 800
CB = 24
STEPS = 2
PAIRS = 64
OWNED = 768
N_BATCH = 32
N_SLAB = 8


def draw_owned_occ(key, part):
    middle = jax.random.permutation(key, jnp.arange(1, NO - 1, dtype=jnp.int32))[:N_BATCH - 2]
    chosen = jnp.concatenate([jnp.array([0, NO - 1], dtype=jnp.int32), middle.astype(jnp.int32)])
    order = jax.random.permutation(jax.random.fold_in(key, 7), N_BATCH)
    return chosen[order].astype(jnp.int32)


def spread_log(key, count, lowest, highest, power):
    unit = jax.random.uniform(key, (count,), jnp.float32)
    unit = unit ** power
    value = jnp.exp(jnp.log(lowest) + (jnp.log(highest) - jnp.log(lowest)) * unit)
    return jnp.clip(value, lowest, highest).astype(jnp.float32)


def draw_occ_energy(key, part):
    key = jax.random.fold_in(key, 11)
    binding = spread_log(key, NO, 0.2, 30.0, 1.0)
    return (0.0 - binding).astype(jnp.float32)


def draw_virt_energy(key, part):
    key = jax.random.fold_in(key, 13)
    return spread_log(key, NV, 0.02, 40.0, 1.0)


def set_ends(result, own_key, least, largest):
    longest = result.shape.index(max(result.shape))
    spots = []
    for shift in (0, 1):
        where = [jax.random.randint(jax.random.fold_in(own_key, axis), (), 0, length) for axis, length in enumerate(result.shape)]
        where[longest] = (where[longest] + shift) % result.shape[longest]
        spots.append(tuple(where))
    return result.at[spots[0]].set(least).at[spots[1]].set(largest)


def levels(rng, shape, pieces, low, largest):
    level = 1.0
    for axis_at, blocks in pieces:
        heights = jax.random.uniform(jax.random.fold_in(jax.random.fold_in(rng, 6), axis_at), (blocks,), jnp.float32, low / len(pieces), largest / len(pieces))
        level = level * jnp.repeat(jnp.exp(heights), shape[axis_at] // blocks).reshape((-1,) + (1,) * (len(shape) - 1 - axis_at))
    return level


def scatter_about(own_key, shape, width, reach, shards=(), held_as=jnp.bfloat16):
    gain = levels(own_key, shape, shards, -0.22, 0.18) if shards else 1.0
    drawn = jax.random.normal(own_key, shape, jnp.float32) * width * gain
    return jnp.minimum(jnp.maximum(drawn, -reach), reach).astype(held_as)


def setup_inputs(seed: int = 0) -> dict:
    key_of = jax.random.split(jax.random.key(seed), 8)
    return {
        "lambda_pairs": scatter_about(key_of[0], (PAIRS, NV, NV), 1.0, 6.0, ((0, 32), (1, 8))),
        "vvvo": scatter_about(key_of[1], (OWNED, NV, NV), NV ** -0.5, 0.21875, ((0, 32), (1, 8))),
        "pair_list": set_ends(jax.random.randint(key_of[2], (PAIRS, 2), 0, NO), jax.random.fold_in(key_of[2], 1), 0, NO - 1).astype(jnp.int32),
        "owned_occ": draw_owned_occ(jax.random.fold_in(key_of[7], 71), 0),
        "step_root": jax.random.randint(key_of[4], (STEPS,), 0, N_BATCH).astype(jnp.int32),
        "occ_energy": draw_occ_energy(jax.random.fold_in(key_of[7], 71), 0),
        "virt_energy": draw_virt_energy(jax.random.fold_in(key_of[7], 71), 0),
    }


def reference(lambda_pairs, vvvo, pair_list, owned_occ, step_root, occ_energy, virt_energy):
    local_b = NV // N_SLAB
    energy_c = virt_energy[:CB]

    def one_pair(pair):
        slot = pair % STEPS
        root = step_root[slot]
        block = lax.dynamic_slice_in_dim(vvvo, (root * CB).astype(jnp.int32), CB, 0)
        amps = lax.dynamic_index_in_dim(lambda_pairs, pair, 0, keepdims=False)
        indices = lax.dynamic_index_in_dim(pair_list, pair, 0, keepdims=False)
        occ_sum = occ_energy[indices[0]] + occ_energy[indices[1]] + occ_energy[owned_occ[root]]
        weighted = jnp.einsum("ad,cbd->cba", amps.astype(jnp.float32), block.astype(jnp.float32))
        denom = occ_sum - energy_c[:, None, None] - virt_energy[None, :, None] - virt_energy[None, None, :]
        triples = (weighted / denom).astype(jnp.bfloat16)
        grouped = triples.reshape(CB, N_SLAB, local_b, NV).astype(jnp.float32)
        blocks = block.reshape(CB, N_SLAB, local_b, NV).astype(jnp.float32)
        parts = jnp.einsum("cgba,cgbd->gad", grouped, blocks)
        return jnp.sum(parts, axis=0)

    return lax.map(one_pair, jnp.arange(N_BATCH * STEPS, dtype=jnp.int32))
```

```python
import functools

import jax
import jax.numpy as jnp
from jax import lax
from jax.experimental import pallas as pl
from jax.experimental.pallas import tpu as pltpu
from jax.sharding import PartitionSpec as P

AXES = ("batch", "slab")
NZ, NYH, NC, NX, NYL = 8, 2, 2, 4, 2


def full_perm(move):
    pairs = []
    for device in range(NZ * NYH * NC * NX * NYL):
        rest, yl = divmod(device, NYL)
        rest, x = divmod(rest, NX)
        rest, core = divmod(rest, NC)
        z, yh = divmod(rest, NYH)
        z, yh, core, x, yl = move(z, yh, core, x, yl)
        target = (((z % NZ) * NYH + yh % NYH) * NC + core % NC) * NX + x % NX
        pairs.append((device, target * NYL + yl % NYL))
    return pairs


SWAP_CORE = full_perm(lambda z, h, c, x, l: (z, h, 1 - c, x, l))
SWAP_YH = full_perm(lambda z, h, c, x, l: (z, 1 - h, c, x, l))
SWAP_YL = full_perm(lambda z, h, c, x, l: (z, h, c, x, 1 - l))
Z_RING = full_perm(lambda z, h, c, x, l: (z + 1 - 2 * c, h, c, x, l))


def x_by(step):
    return full_perm(lambda z, h, c, x, l: (z, h, c, x + step, l))


def send(array, perm):
    return lax.ppermute(array, AXES, perm)


def triples_kernel(n_pieces, has_prev, chunk, *refs):
    lam_ref, base_ref, ea_ref = refs[:3]
    pieces = refs[3 : 3 + n_pieces]
    out_ref, block_ref = refs[len(refs) - 2 :]

    @pl.when(pl.program_id(0) == 0)
    def _():
        at = 0
        for piece in pieces:
            rows = piece.shape[0]
            block_ref[at : at + rows, :] = piece[...]
            at += rows

    if has_prev:
        out_ref[...] = refs[3 + n_pieces][...]
    lam = lam_ref[...]
    n_a = lam.shape[0]
    part = n_a // 4
    rows = block_ref.shape[0]
    for at in range(0, rows, chunk):
        size = min(chunk, rows - at)
        block = block_ref[at : at + size, :]
        weighted = lax.dot_general(
            lam, block, (((1,), (1,)), ((), ())), preferred_element_type=jnp.float32
        )
        divided = []
        for k in range(4):
            denom = base_ref[k % 2 : k % 2 + 1, at : at + size] - ea_ref[k * part : (k + 1) * part, :]
            divided.append(weighted[k * part : (k + 1) * part] / denom)
        triples = jnp.concatenate(divided, axis=0).astype(jnp.bfloat16)
        share = jnp.dot(triples, block, preferred_element_type=jnp.float32)
        if at == 0 and not has_prev:
            out_ref[...] = share
        else:
            out_ref[...] += share


def triples_call(lam, base, ea, pieces, prev):
    rows = sum(p.shape[0] for p in pieces)
    n_a, width = lam.shape
    tile = n_a // 2
    padded = -(-rows // 128) * 128
    base = jnp.pad(base, ((0, 0), (0, padded - rows)), constant_values=1.0)
    tile_spec = pl.BlockSpec((tile, width), lambda g: (g, 0))
    in_specs = [
        tile_spec,
        pl.BlockSpec((2, padded), lambda g: (0, 0)),
        pl.BlockSpec((tile, 1), lambda g: (g, 0)),
    ]
    in_specs += [pl.BlockSpec(p.shape, lambda g: (0, 0)) for p in pieces]
    args = [lam, base, ea, *pieces]
    if prev is not None:
        in_specs.append(tile_spec)
        args.append(prev)
    return pl.pallas_call(
        functools.partial(triples_kernel, len(pieces), prev is not None, 512),
        grid=(2,),
        in_specs=in_specs,
        out_specs=tile_spec,
        out_shape=jax.ShapeDtypeStruct((n_a, width), jnp.float32),
        scratch_shapes=[pltpu.VMEM((rows, width), jnp.bfloat16)],
        compiler_params=pltpu.CompilerParams(vmem_limit_bytes=56 * 1024 * 1024),
        cost_estimate=pl.CostEstimate(
            flops=4 * rows * n_a * width,
            bytes_accessed=2 * rows * width + 10 * n_a * width,
            transcendentals=0,
        ),
    )(*args)


def body(lambda_pairs, vvvo, pair_list, owned_occ, step_root, occ_energy, virt_energy):
    window, local_b, width = vvvo.shape
    n_rows = window * local_b
    batch_pos = lax.axis_index("batch")
    slab_pos = lax.axis_index("slab")
    core = batch_pos % NC
    yh = (batch_pos // NC) % NYH
    z = batch_pos // (NC * NYH)
    x = slab_pos // NYL
    yl = slab_pos % NYL
    up = core == 0
    ahead_sign = 1 - 2 * core
    root_own = jnp.where(up, step_root[0], step_root[1])
    root_other = jnp.where(up, step_root[1], step_root[0])

    flat = vvvo.transpose(1, 0, 2).reshape(n_rows, width)
    piece = -(-n_rows // (NZ * 16)) * 16
    half = -(-piece // 32) * 16
    far = NZ // 2

    def ahead(sign, steps):
        start = jnp.minimum((z + sign * steps) % NZ * piece, n_rows - piece)
        if steps < far:
            return lax.dynamic_slice_in_dim(flat, start, piece)
        start = start + jnp.where(sign > 0, 0, piece - half)
        return lax.dynamic_slice_in_dim(flat, start, half)

    from_other = send(
        jnp.concatenate([ahead(-ahead_sign, k) for k in range(far + 1)]), SWAP_CORE
    )

    def inject(root, steps):
        at = steps * piece
        theirs = from_other[at : at + (piece if steps < far else half)]
        return jnp.where(root % NC == core, ahead(ahead_sign, steps), theirs)

    def on_root(root):
        return root // NC == batch_pos // NC

    got_own = send(inject(root_own, far), Z_RING)
    got_other = send(inject(root_other, far), Z_RING)
    rest = piece - half
    for k in range(far - 1, 0, -1):
        if k == far - 1:
            got_own, got_other = [
                jnp.where(
                    up, jnp.concatenate([g, g[half - rest :]]), jnp.concatenate([g[:rest], g])
                )
                for g in (got_own, got_other)
            ]
        got_own = send(jnp.where(on_root(root_own), inject(root_own, k), got_own), Z_RING)
        got_other = send(jnp.where(on_root(root_other), inject(root_other, k), got_other), Z_RING)
    crossed = send(got_other, SWAP_CORE)
    apart = (z - root_own // (NC * NYH)) % NZ
    from_below = (apart < far) | ((apart == far) & (jnp.arange(piece) < half))[:, None]
    mine = jnp.where(
        on_root(root_own), inject(root_own, 0), jnp.where(from_below == up, got_own, crossed)
    )
    here = jnp.where((root_own // NC) % NYH == yh, mine, send(mine, SWAP_YH))

    own = lax.dynamic_index_in_dim(lambda_pairs, core, 0, keepdims=False)
    give = lax.dynamic_index_in_dim(lambda_pairs, 1 - core, 0, keepdims=False)
    lam = jnp.stack([own, send(give, SWAP_CORE)])
    lam = jnp.stack([lam, send(lam, SWAP_YL)], axis=1).reshape(2 * NYL * local_b, width)
    lam = jnp.concatenate([lam, send(lam, x_by(-1)), send(lam, x_by(-2)), send(lam, x_by(1))])

    pair_sum = occ_energy[pair_list[:, 0]] + occ_energy[pair_list[:, 1]]
    own_sum = lax.dynamic_index_in_dim(pair_sum, core, 0)
    give_sum = lax.dynamic_index_in_dim(pair_sum, 1 - core, 0)
    occ_sum = jnp.concatenate([own_sum, send(give_sum, SWAP_CORE)]) + occ_energy[owned_occ[root_own]]
    energy_b = lax.dynamic_slice_in_dim(virt_energy, slab_pos * local_b, local_b)
    energy_c = virt_energy[:window]
    base = ((occ_sum[:, None, None] - energy_c) - energy_b[:, None]).reshape(2, n_rows)
    last = (NZ - 1) * piece
    spare = NZ * piece - n_rows
    base = jnp.concatenate(
        [base[:, :last], jnp.full((2, spare), jnp.inf, jnp.float32), base[:, last:]], axis=1
    ).reshape(2, NZ, piece)
    base = lax.dynamic_slice_in_dim(jnp.concatenate([base, base], axis=1), z, NZ, axis=1)
    base = jnp.where(up, jnp.roll(base[:, ::-1], 1, axis=1), base)
    ea = virt_energy.reshape(NX, NYL, local_b)
    ea = jnp.where(yl == 0, ea, ea[:, ::-1])
    ea = lax.dynamic_slice_in_dim(jnp.concatenate([ea, ea], axis=0), x, NX, axis=0)
    ea = jnp.stack([ea, ea], axis=1).reshape(lam.shape[0], 1)

    here, lam, base, ea = lax.optimization_barrier((here, lam, base, ea))
    ring_own, ring_other = [here], [send(here, SWAP_CORE)]
    for _ in range(far - 1):
        ring_own.append(send(ring_own[-1], Z_RING))
        ring_other.append(send(ring_other[-1], Z_RING))
    crossed = [send(r, SWAP_CORE) for r in ring_other[1:]]

    def far_half(array):
        return lax.dynamic_slice_in_dim(array, jnp.where(up, 0, rest), half)

    far_own = send(far_half(ring_own[-1]), Z_RING)
    far_other = send(send(far_half(ring_other[-1]), Z_RING), SWAP_CORE)
    far_piece = jnp.where(
        up,
        jnp.concatenate([far_own, far_other[half - rest :]]),
        jnp.concatenate([far_other, far_own[half - rest :]]),
    )

    def base_of(order):
        return jnp.concatenate([base[:, k] for k in order], axis=1)

    total = triples_call(lam, base_of([0, 1, 7]), ea, [here, ring_own[1], crossed[0]], None)
    total = triples_call(lam, base_of([2, 6]), ea, [ring_own[2], crossed[1]], total)
    total = triples_call(
        lam, base_of([3, 5, 4]), ea, [ring_own[3], crossed[2], far_piece], total
    )

    total = total.reshape(NX, 2 * NYL * local_b, width)
    rows = total[0] + send(total[1], x_by(1)) + send(total[2], x_by(2)) + send(total[3], x_by(-1))
    rows = rows.reshape(2, NYL, local_b, width)
    rows = rows[:, 0] + send(rows[:, 1], SWAP_YL)
    other = send(rows[1], SWAP_CORE)
    return jnp.where(up, jnp.stack([rows[0], other]), jnp.stack([other, rows[0]]))


def solution(mesh):
    placed = (
        P("batch", "slab", None),
        P("batch", "slab", None),
        P("batch", None),
        P(),
        P(),
        P(),
        P(),
    )
    return jax.shard_map(
        body, mesh=mesh, in_specs=placed, out_specs=P("batch", "slab", None), check_vma=False
    )
```

```python
import functools

import jax
import jax.numpy as jnp
from jax import lax
from jax.experimental import pallas as pl
from jax.experimental.pallas import tpu as pltpu
from jax.sharding import PartitionSpec as P

AXES = ("batch", "slab")
NZ, NYH, NC, NX, NYL = 8, 2, 2, 4, 2


def full_perm(move):
    pairs = []
    for device in range(NZ * NYH * NC * NX * NYL):
        rest, yl = divmod(device, NYL)
        rest, x = divmod(rest, NX)
        rest, core = divmod(rest, NC)
        z, yh = divmod(rest, NYH)
        z, yh, core, x, yl = move(z, yh, core, x, yl)
        target = (((z % NZ) * NYH + yh % NYH) * NC + core % NC) * NX + x % NX
        pairs.append((device, target * NYL + yl % NYL))
    return pairs


SWAP_CORE = full_perm(lambda z, h, c, x, l: (z, h, 1 - c, x, l))
SWAP_YH = full_perm(lambda z, h, c, x, l: (z, 1 - h, c, x, l))
SWAP_YL = full_perm(lambda z, h, c, x, l: (z, h, c, x, 1 - l))
Z_RING = full_perm(lambda z, h, c, x, l: (z + 1 - 2 * c, h, c, x, l))


def x_by(step):
    return full_perm(lambda z, h, c, x, l: (z, h, c, x + step, l))


def send(array, perm):
    return lax.ppermute(array, AXES, perm)


def triples_kernel(n_pieces, has_prev, last, chunk, *refs):
    lam_ref, base_ref, ea_ref = refs[:3]
    pieces = refs[3 : 3 + n_pieces]
    block_ref = refs[-1]
    if last:
        kept_ref, shares_ref, out_ref = refs[len(refs) - 4 : len(refs) - 1]
    else:
        out_ref = refs[-2]

    @pl.when(pl.program_id(0) == 0)
    def _():
        at = 0
        for piece in pieces:
            rows = piece.shape[0]
            block_ref[at : at + rows, :] = piece[...]
            at += rows

    if has_prev:
        out_ref[...] = refs[3 + n_pieces][...]
    lam = lam_ref[...]
    n_a = lam.shape[0]
    part = n_a // 4
    rows = block_ref.shape[0]
    for at in range(0, rows, chunk):
        size = min(chunk, rows - at)
        block = block_ref[at : at + size, :]
        weighted = lax.dot_general(
            lam, block, (((1,), (1,)), ((), ())), preferred_element_type=jnp.float32
        )
        divided = []
        for k in range(4):
            denom = base_ref[k % 2 : k % 2 + 1, at : at + size] - ea_ref[k * part : (k + 1) * part, :]
            inverse = pl.reciprocal(denom, approx=True)
            inverse = inverse * (2.0 - denom * inverse)
            divided.append(weighted[k * part : (k + 1) * part] * inverse)
        triples = jnp.concatenate(divided, axis=0).astype(jnp.bfloat16)
        share = jnp.dot(triples, block, preferred_element_type=jnp.float32)
        if at == 0 and not has_prev:
            out_ref[...] = share
        else:
            out_ref[...] += share

    if last:

        @pl.when(pl.program_id(0) == 0)
        def _():
            kept_ref[...] = out_ref[: kept_ref.shape[0], :]

        width = out_ref.shape[1]
        pad = shares_ref.shape[1] - width
        for at in range(0, n_a, 80):
            part_sum = out_ref[at : at + 80, :]
            top = jnp.maximum(jnp.max(jnp.abs(part_sum), axis=1, keepdims=True), 2.0**-110)
            exponent = jnp.ceil(jnp.log(top * 1.0001) * 1.4426950408889634) - 15.0
            coded = jnp.floor(part_sum * jnp.exp2(-exponent) + 0.5)
            coded = jnp.concatenate([coded, jnp.broadcast_to(exponent, (80, pad))], axis=1)
            shares_ref[at : at + 80, :] = coded.astype(jnp.int32).astype(jnp.int16)


def triples_call(lam, base, ea, pieces, prev, last=False):
    rows = sum(p.shape[0] for p in pieces)
    n_a, width = lam.shape
    tile = n_a // 2
    padded = -(-rows // 128) * 128
    base = jnp.pad(base, ((0, 0), (0, padded - rows)), constant_values=1.0)
    tile_spec = pl.BlockSpec((tile, width), lambda g: (g, 0))
    in_specs = [
        tile_spec,
        pl.BlockSpec((2, padded), lambda g: (0, 0)),
        pl.BlockSpec((tile, 1), lambda g: (g, 0)),
    ]
    in_specs += [pl.BlockSpec(p.shape, lambda g: (0, 0)) for p in pieces]
    args = [lam, base, ea, *pieces]
    if prev is not None:
        in_specs.append(tile_spec)
        args.append(prev)
    out_specs, out_shape = tile_spec, jax.ShapeDtypeStruct((n_a, width), jnp.float32)
    scratch = [pltpu.VMEM((rows, width), jnp.bfloat16)]
    if last:
        wide = -(-(width + 1) // 128) * 128
        out_specs = [
            pl.BlockSpec((n_a // NX, width), lambda g: (0, 0)),
            pl.BlockSpec((tile, wide), lambda g: (g, 0)),
        ]
        out_shape = [
            jax.ShapeDtypeStruct((n_a // NX, width), jnp.float32),
            jax.ShapeDtypeStruct((n_a, wide), jnp.int16),
        ]
        scratch = [pltpu.VMEM((tile, width), jnp.float32)] + scratch
    return pl.pallas_call(
        functools.partial(triples_kernel, len(pieces), prev is not None, last, 512),
        grid=(2,),
        in_specs=in_specs,
        out_specs=out_specs,
        out_shape=out_shape,
        scratch_shapes=scratch,
        compiler_params=pltpu.CompilerParams(vmem_limit_bytes=56 * 1024 * 1024),
        cost_estimate=pl.CostEstimate(
            flops=4 * rows * n_a * width,
            bytes_accessed=2 * rows * width + 10 * n_a * width,
            transcendentals=0,
        ),
    )(*args)


def body(lambda_pairs, vvvo, pair_list, owned_occ, step_root, occ_energy, virt_energy):
    window, local_b, width = vvvo.shape
    n_rows = window * local_b
    batch_pos = lax.axis_index("batch")
    slab_pos = lax.axis_index("slab")
    core = batch_pos % NC
    yh = (batch_pos // NC) % NYH
    z = batch_pos // (NC * NYH)
    x = slab_pos // NYL
    yl = slab_pos % NYL
    up = core == 0
    ahead_sign = 1 - 2 * core
    root_own = jnp.where(up, step_root[0], step_root[1])
    root_other = jnp.where(up, step_root[1], step_root[0])

    own = lax.dynamic_index_in_dim(lambda_pairs, core, 0, keepdims=False)
    give = lax.dynamic_index_in_dim(lambda_pairs, 1 - core, 0, keepdims=False)
    lam = jnp.stack([own, send(give, SWAP_CORE)])
    lam = jnp.stack([lam, send(lam, SWAP_YL)], axis=1).reshape(2 * NYL * local_b, width)

    flat = vvvo.transpose(1, 0, 2).reshape(n_rows, width)
    piece = -(-n_rows // (NZ * 16)) * 16
    half = -(-piece // 32) * 16
    far = NZ // 2

    def ahead(sign, steps):
        start = jnp.minimum((z + sign * steps) % NZ * piece, n_rows - piece)
        if steps < far:
            return lax.dynamic_slice_in_dim(flat, start, piece)
        start = start + jnp.where(sign > 0, 0, piece - half)
        return lax.dynamic_slice_in_dim(flat, start, half)

    far_swapped = send(ahead(-ahead_sign, far), SWAP_CORE)
    swapped = send(
        jnp.concatenate([ahead(-ahead_sign, k) for k in range(far - 1, -1, -1)]), SWAP_CORE
    )

    def inject(root, steps):
        if steps == far:
            theirs = far_swapped
        else:
            theirs = swapped[(far - 1 - steps) * piece : (far - steps) * piece]
        return jnp.where(root % NC == core, ahead(ahead_sign, steps), theirs)

    def on_root(root):
        return root // NC == batch_pos // NC

    def after(array, earlier):
        return lax.optimization_barrier((array, earlier))[0]

    rest = piece - half

    def widen(array):
        above = jnp.concatenate([array, array[half - rest :]])
        return jnp.where(up, above, jnp.concatenate([array[:rest], array]))

    give_own = inject(root_own, far)
    got_own = send(give_own, Z_RING)
    got_other = send(inject(root_other, far), Z_RING)
    for k in range(far - 1, 0, -1):
        if k == far - 1:
            got_own, got_other = widen(got_own), widen(got_other)
        elif k == far - 2:
            got_own, lam = lax.optimization_barrier((got_own, lam))
        give_own = jnp.where(on_root(root_own), inject(root_own, k), got_own)
        got_own = send(give_own, Z_RING)
        got_other = after(got_other, give_own)
        got_other = send(jnp.where(on_root(root_other), inject(root_other, k), got_other), Z_RING)
    crossed = send(got_other, SWAP_CORE)
    apart = (z - root_own // (NC * NYH)) % NZ
    from_below = (apart < far) | ((apart == far) & (jnp.arange(piece) < half))[:, None]
    mine = jnp.where(
        on_root(root_own), inject(root_own, 0), jnp.where(from_below == up, got_own, crossed)
    )
    here = jnp.where((root_own // NC) % NYH == yh, mine, send(mine, SWAP_YH))

    lam = jnp.concatenate([lam, send(lam, x_by(-1)), send(lam, x_by(-2)), send(lam, x_by(1))])

    pair_sum = occ_energy[pair_list[:, 0]] + occ_energy[pair_list[:, 1]]
    own_sum = lax.dynamic_index_in_dim(pair_sum, core, 0)
    give_sum = lax.dynamic_index_in_dim(pair_sum, 1 - core, 0)
    occ_sum = jnp.concatenate([own_sum, send(give_sum, SWAP_CORE)]) + occ_energy[owned_occ[root_own]]
    energy_b = lax.dynamic_slice_in_dim(virt_energy, slab_pos * local_b, local_b)
    energy_c = virt_energy[:window]
    base = ((occ_sum[:, None, None] - energy_c) - energy_b[:, None]).reshape(2, n_rows)
    last = (NZ - 1) * piece
    spare = NZ * piece - n_rows
    base = jnp.concatenate(
        [base[:, :last], jnp.full((2, spare), 1e30, jnp.float32), base[:, last:]], axis=1
    ).reshape(2, NZ, piece)
    base = lax.dynamic_slice_in_dim(jnp.concatenate([base, base], axis=1), z, NZ, axis=1)
    base = jnp.where(up, jnp.roll(base[:, ::-1], 1, axis=1), base)
    ea = virt_energy.reshape(NX, NYL, local_b)
    ea = jnp.where(yl == 0, ea, ea[:, ::-1])
    ea = lax.dynamic_slice_in_dim(jnp.concatenate([ea, ea], axis=0), x, NX, axis=0)
    ea = jnp.stack([ea, ea], axis=1).reshape(lam.shape[0], 1)

    def base_of(order):
        return jnp.concatenate([base[:, k] for k in order], axis=1)

    here, lam, base, ea = lax.optimization_barrier((here, lam, base, ea))
    ring_own, ring_other, crossed = [here], [send(here, SWAP_CORE)], []
    total = None
    for k in range(1, far):
        if k == far - 1:
            ring_own[-1], ring_other[-1], _ = lax.optimization_barrier(
                (ring_own[-1], ring_other[-1], first)
            )
        ring_own.append(send(ring_own[-1], Z_RING))
        ring_other.append(send(ring_other[-1], Z_RING))
        crossed.append(send(ring_other[-1], SWAP_CORE))
        if k == 1:
            first = triples_call(lam, base_of([0, 1, 7]), ea, [here, ring_own[1], crossed[0]], None)
        elif k == 2:
            total = triples_call(lam, base_of([2, 6]), ea, [ring_own[2], crossed[1]], first)
    ring_own[-1], ring_other[-1], total = lax.optimization_barrier(
        (ring_own[-1], ring_other[-1], total)
    )

    def far_half(array):
        return lax.dynamic_slice_in_dim(array, jnp.where(up, 0, rest), half)

    far_own = send(far_half(ring_own[-1]), Z_RING)
    far_other = send(send(far_half(ring_other[-1]), Z_RING), SWAP_CORE)
    far_piece = jnp.where(
        up,
        jnp.concatenate([far_own, far_other[half - rest :]]),
        jnp.concatenate([far_other, far_own[half - rest :]]),
    )

    kept, shares = triples_call(
        lam, base_of([3, 5, 4]), ea, [ring_own[3], crossed[2], far_piece], total, last=True
    )
    shares = shares.reshape(NX, 2 * NYL * local_b, -1)
    rows = kept
    for step in range(1, NX):
        got = send(shares[step], x_by(step)).astype(jnp.float32)
        rows = rows + got[:, :width] * jnp.exp2(got[:, width : width + 1])
    rows = rows.reshape(2, NYL, local_b, width)
    rows = rows[:, 0] + send(rows[:, 1], SWAP_YL)
    other = send(rows[1], SWAP_CORE)
    return jnp.where(up, jnp.stack([rows[0], other]), jnp.stack([other, rows[0]]))


def solution(mesh):
    placed = (
        P("batch", "slab", None),
        P("batch", "slab", None),
        P("batch", None),
        P(),
        P(),
        P(),
        P(),
    )
    return jax.shard_map(
        body, mesh=mesh, in_specs=placed, out_specs=P("batch", "slab", None), check_vma=False
    )
```

```python
import functools

import jax
import jax.numpy as jnp
from jax import lax
from jax.experimental import pallas as pl
from jax.experimental.pallas import tpu as pltpu
from jax.sharding import PartitionSpec as P

AXES = ("batch", "slab")
NZ, NYH, NC, NX, NYL = 8, 2, 2, 4, 2


def full_perm(move):
    pairs = []
    for device in range(NZ * NYH * NC * NX * NYL):
        rest, yl = divmod(device, NYL)
        rest, x = divmod(rest, NX)
        rest, core = divmod(rest, NC)
        z, yh = divmod(rest, NYH)
        z, yh, core, x, yl = move(z, yh, core, x, yl)
        target = (((z % NZ) * NYH + yh % NYH) * NC + core % NC) * NX + x % NX
        pairs.append((device, target * NYL + yl % NYL))
    return pairs


SWAP_CORE = full_perm(lambda z, h, c, x, l: (z, h, 1 - c, x, l))
SWAP_YH = full_perm(lambda z, h, c, x, l: (z, 1 - h, c, x, l))
SWAP_YL = full_perm(lambda z, h, c, x, l: (z, h, c, x, 1 - l))
Z_RING = full_perm(lambda z, h, c, x, l: (z + 1 - 2 * c, h, c, x, l))


def x_by(step):
    return full_perm(lambda z, h, c, x, l: (z, h, c, x + step, l))


def send(array, perm):
    return lax.ppermute(array, AXES, perm)


def triples_kernel(n_pieces, has_prev, last, chunk, *refs):
    base_ref, ea_ref = refs[:2]
    lam_refs = refs[2 : 2 + NX]
    pieces = refs[2 + NX : 2 + NX + n_pieces]
    lam_ref, block_ref = refs[len(refs) - 2 :]
    if last:
        kept_ref, shares_ref, out_ref = refs[len(refs) - 5 : len(refs) - 2]
    else:
        out_ref = refs[len(refs) - 3]

    @pl.when(pl.program_id(0) == 0)
    def _():
        at = 0
        for piece in pieces:
            rows = piece.shape[0]
            block_ref[at : at + rows, :] = piece[...]
            at += rows

    for g in range(2):

        @pl.when(pl.program_id(0) == g)
        def _():
            for k in range(2):
                rows = lam_refs[2 * g + k].shape[0]
                lam_ref[k * rows : (k + 1) * rows, :] = lam_refs[2 * g + k][...]

    if has_prev:
        out_ref[...] = refs[2 + NX + n_pieces][...]
    lam = lam_ref[...]
    n_a = lam.shape[0]
    part = n_a // 4
    rows = block_ref.shape[0]
    for at in range(0, rows, chunk):
        size = min(chunk, rows - at)
        block = block_ref[at : at + size, :]
        weighted = lax.dot_general(
            lam, block, (((1,), (1,)), ((), ())), preferred_element_type=jnp.float32
        )
        divided = []
        for k in range(4):
            denom = base_ref[k % 2 : k % 2 + 1, at : at + size] - ea_ref[k * part : (k + 1) * part, :]
            inverse = pl.reciprocal(denom, approx=True)
            inverse = inverse * (2.0 - denom * inverse)
            divided.append(weighted[k * part : (k + 1) * part] * inverse)
        triples = jnp.concatenate(divided, axis=0).astype(jnp.bfloat16)
        share = jnp.dot(triples, block, preferred_element_type=jnp.float32)
        if at == 0 and not has_prev:
            out_ref[...] = share
        else:
            out_ref[...] += share

    if last:

        @pl.when(pl.program_id(0) == 0)
        def _():
            kept_ref[...] = out_ref[: kept_ref.shape[0], :]

        width = out_ref.shape[1]
        pad = shares_ref.shape[1] - width
        for at in range(0, n_a, 80):
            part_sum = out_ref[at : at + 80, :]
            top = jnp.maximum(jnp.max(jnp.abs(part_sum), axis=1, keepdims=True), 2.0**-110)
            exponent = jnp.ceil(jnp.log(top * 1.0001) * 1.4426950408889634) - 15.0
            coded = jnp.floor(part_sum * jnp.exp2(-exponent) + 0.5)
            coded = jnp.concatenate([coded, jnp.broadcast_to(exponent, (80, pad))], axis=1)
            shares_ref[at : at + 80, :] = coded.astype(jnp.int32).astype(jnp.int16)


def triples_call(lams, base, ea, pieces, prev, last):
    rows = sum(p.shape[0] for p in pieces)
    n_a, width = NX * lams[0].shape[0], lams[0].shape[1]
    tile = n_a // 2
    padded = -(-rows // 128) * 128
    base = jnp.pad(base, ((0, 0), (0, padded - rows)), constant_values=1.0)
    tile_spec = pl.BlockSpec((tile, width), lambda g: (g, 0))
    in_specs = [
        pl.BlockSpec((2, padded), lambda g: (0, 0)),
        pl.BlockSpec((tile, 1), lambda g: (g, 0)),
    ]
    in_specs += [pl.BlockSpec(p.shape, lambda g: (0, 0)) for p in [*lams, *pieces]]
    args = [base, ea, *lams, *pieces]
    if prev is not None:
        in_specs.append(tile_spec)
        args.append(prev)
    out_specs, out_shape = tile_spec, jax.ShapeDtypeStruct((n_a, width), jnp.float32)
    scratch = [pltpu.VMEM((tile, width), jnp.bfloat16), pltpu.VMEM((rows, width), jnp.bfloat16)]
    if last:
        wide = -(-(width + 1) // 128) * 128
        out_specs = [
            pl.BlockSpec((n_a // NX, width), lambda g: (0, 0)),
            pl.BlockSpec((tile, wide), lambda g: (g, 0)),
        ]
        out_shape = [
            jax.ShapeDtypeStruct((n_a // NX, width), jnp.float32),
            jax.ShapeDtypeStruct((n_a, wide), jnp.int16),
        ]
        scratch = [pltpu.VMEM((tile, width), jnp.float32)] + scratch
    return pl.pallas_call(
        functools.partial(triples_kernel, len(pieces), prev is not None, last, 512),
        grid=(2,),
        in_specs=in_specs,
        out_specs=out_specs,
        out_shape=out_shape,
        scratch_shapes=scratch,
        compiler_params=pltpu.CompilerParams(vmem_limit_bytes=56 * 1024 * 1024),
        cost_estimate=pl.CostEstimate(
            flops=4 * rows * n_a * width,
            bytes_accessed=2 * rows * width + 10 * n_a * width,
            transcendentals=0,
        ),
    )(*args)


def body(lambda_pairs, vvvo, pair_list, owned_occ, step_root, occ_energy, virt_energy):
    window, local_b, width = vvvo.shape
    n_rows = window * local_b
    batch_pos = lax.axis_index("batch")
    slab_pos = lax.axis_index("slab")
    core = batch_pos % NC
    yh = (batch_pos // NC) % NYH
    z = batch_pos // (NC * NYH)
    x = slab_pos // NYL
    yl = slab_pos % NYL
    up = core == 0
    ahead_sign = 1 - 2 * core
    root_own = jnp.where(up, step_root[0], step_root[1])
    root_other = jnp.where(up, step_root[1], step_root[0])

    own = lax.dynamic_index_in_dim(lambda_pairs, core, 0, keepdims=False)
    give = lax.dynamic_index_in_dim(lambda_pairs, 1 - core, 0, keepdims=False)
    lam = jnp.stack([own, send(give, SWAP_CORE)])
    lam = jnp.stack([lam, send(lam, SWAP_YL)], axis=1).reshape(2 * NYL * local_b, width)

    piece = -(-n_rows // (NZ * 16)) * 16

    pair_sum = occ_energy[pair_list[:, 0]] + occ_energy[pair_list[:, 1]]
    own_sum = lax.dynamic_index_in_dim(pair_sum, core, 0)
    give_sum = lax.dynamic_index_in_dim(pair_sum, 1 - core, 0)
    occ_sum = jnp.concatenate([own_sum, send(give_sum, SWAP_CORE)]) + occ_energy[owned_occ[root_own]]
    energy_b = lax.dynamic_slice_in_dim(virt_energy, slab_pos * local_b, local_b)
    energy_c = virt_energy[:window]
    base = ((occ_sum[:, None, None] - energy_c) - energy_b[:, None]).reshape(2, n_rows)
    last = (NZ - 1) * piece
    spare = NZ * piece - n_rows
    base = jnp.concatenate(
        [base[:, :last], jnp.full((2, spare), 1e30, jnp.float32), base[:, last:]], axis=1
    ).reshape(2, NZ, piece)
    base = lax.dynamic_slice_in_dim(jnp.concatenate([base, base], axis=1), z, NZ, axis=1)
    base = jnp.where(up, jnp.roll(base[:, ::-1], 1, axis=1), base)
    ea = virt_energy.reshape(NX, NYL, local_b)
    ea = jnp.where(yl == 0, ea, ea[:, ::-1])
    ea = lax.dynamic_slice_in_dim(jnp.concatenate([ea, ea], axis=0), x, NX, axis=0)
    ea = jnp.stack([ea, ea], axis=1).reshape(NX * 2 * NYL * local_b, 1)

    flat = vvvo.transpose(1, 0, 2).reshape(n_rows, width)
    far = NZ // 2

    def ahead(sign, steps):
        start = jnp.minimum((z + sign * steps) % NZ * piece, n_rows - piece)
        return lax.dynamic_slice_in_dim(flat, start, piece)

    swapped = {k: send(ahead(-ahead_sign, k), SWAP_CORE) for k in range(far, -1, -1)}

    def inject(root, steps, theirs):
        return jnp.where(root % NC == core, ahead(ahead_sign, steps), theirs)

    def on_root(root):
        return root // NC == batch_pos // NC

    def after(array, earlier):
        return lax.optimization_barrier((array, earlier))[0]

    def both(*arrays):
        return lax.optimization_barrier(arrays)

    give_own = inject(root_own, far, swapped[far])
    got_own = send(give_own, Z_RING)
    give_other = got_other = None
    for k in range(far - 1, 0, -1):
        if give_other is not None:
            got_own = after(got_own, give_other)
        if k == far - 2:
            got_own, lam = both(got_own, lam)
            lam_x = {step: send(lam, x_by(-step)) for step in (1, NX - 1, 2)}
        elif k == far - 3:
            got_own, lam_x[1], lam_x[NX - 1], base, ea = both(
                got_own, lam_x[1], lam_x[NX - 1], base, ea
            )
        give_own = jnp.where(on_root(root_own), inject(root_own, k, swapped[k]), got_own)
        got_own = send(give_own, Z_RING)
        if got_other is None:
            give_other = inject(root_other, k, after(swapped[k], give_own))
        else:
            got_other = after(got_other, give_own)
            give_other = jnp.where(
                on_root(root_other), inject(root_other, k, swapped[k]), got_other
            )
        got_other = send(give_other, Z_RING)
    crossed = send(got_other, SWAP_CORE)
    along = ((z - root_own // (NC * NYH)) * ahead_sign) % NZ
    mine = jnp.where(
        on_root(root_own),
        inject(root_own, 0, swapped[0]),
        jnp.where(along <= far, got_own, crossed),
    )
    here = jnp.where((root_own // NC) % NYH == yh, mine, send(mine, SWAP_YH))
    lams = [lam, lam_x[1], lam_x[2], lam_x[NX - 1]]

    def base_of(order):
        return jnp.concatenate([base[:, k] for k in order], axis=1)

    def add_pieces(total, order, pieces, last=False):
        return triples_call(lams, base_of(order), ea, pieces, total, last)

    here, *lams = both(here, *lams)
    own, other, crossed = here, send(here, SWAP_CORE), here
    total = None
    for k in range(1, far):
        next_own, next_other = send(own, Z_RING), send(other, Z_RING)
        if k == 1:
            total = add_pieces(None, [0], [here])
        else:
            total = add_pieces(total, [k - 1, NZ + 1 - k], [own, crossed])
        own, other, total = both(next_own, next_other, total)
        crossed = send(other, SWAP_CORE)
    farthest = send(own, Z_RING)
    total = add_pieces(total, [far - 1, far + 1], [own, crossed])

    kept, shares = add_pieces(total, [far], [farthest], last=True)
    shares = shares.reshape(NX, 2 * NYL * local_b, -1)
    rows = kept
    for step in range(1, NX):
        got = send(shares[step], x_by(step)).astype(jnp.float32)
        rows = rows + got[:, :width] * jnp.exp2(got[:, width : width + 1])
    rows = rows.reshape(2, NYL, local_b, width)
    rows = rows[:, 0] + send(rows[:, 1], SWAP_YL)
    other = send(rows[1], SWAP_CORE)
    return jnp.where(up, jnp.stack([rows[0], other]), jnp.stack([other, rows[0]]))


def solution(mesh):
    placed = (
        P("batch", "slab", None),
        P("batch", "slab", None),
        P("batch", None),
        P(),
        P(),
        P(),
        P(),
    )
    return jax.shard_map(
        body, mesh=mesh, in_specs=placed, out_specs=P("batch", "slab", None), check_vma=False
    )
```

```python
import functools

import jax
import jax.numpy as jnp
from jax import lax
from jax.experimental import pallas as pl
from jax.experimental.pallas import tpu as pltpu
from jax.sharding import PartitionSpec as P

AXES = ("batch", "slab")
NZ, NYH, NC, NX, NYL = 8, 2, 2, 4, 2


def full_perm(move):
    pairs = []
    for device in range(NZ * NYH * NC * NX * NYL):
        rest, yl = divmod(device, NYL)
        rest, x = divmod(rest, NX)
        rest, core = divmod(rest, NC)
        z, yh = divmod(rest, NYH)
        z, yh, core, x, yl = move(z, yh, core, x, yl)
        target = (((z % NZ) * NYH + yh % NYH) * NC + core % NC) * NX + x % NX
        pairs.append((device, target * NYL + yl % NYL))
    return pairs


SWAP_CORE = full_perm(lambda z, h, c, x, l: (z, h, 1 - c, x, l))
SWAP_YH = full_perm(lambda z, h, c, x, l: (z, 1 - h, c, x, l))
SWAP_YL = full_perm(lambda z, h, c, x, l: (z, h, c, x, 1 - l))
Z_RING = full_perm(lambda z, h, c, x, l: (z + 1 - 2 * c, h, c, x, l))


def x_by(step):
    return full_perm(lambda z, h, c, x, l: (z, h, c, x + step, l))


def send(array, perm):
    return lax.ppermute(array, AXES, perm)


def encode(value, wide):
    top = jnp.maximum(jnp.max(jnp.abs(value), axis=1, keepdims=True), 2.0**-110)
    exponent = jnp.ceil(jnp.log(top * 1.0001) * 1.4426950408889634) - 15.0
    coded = jnp.floor(value * jnp.exp2(-exponent) + 0.5)
    tail = jnp.broadcast_to(exponent, (value.shape[0], wide - value.shape[1]))
    return jnp.concatenate([coded, tail], axis=1).astype(jnp.int32).astype(jnp.int16)


def decode(coded, width):
    coded = coded.astype(jnp.float32)
    return coded[:, :width] * jnp.exp2(coded[:, width : width + 1])


def triples_kernel(n_pieces, first, last, chunk, *refs):
    base_ref, ea_ref = refs[:2]
    if first:
        lam_refs = refs[2 : 2 + NX]
        at = 2 + NX
    else:
        lam_ref, prev_ref = refs[2:4]
        at = 4
    pieces = refs[at : at + n_pieces]
    outs = refs[at + n_pieces : len(refs) - 1]
    block_ref = refs[-1]
    g = pl.program_id(0)

    @pl.when(g == 0)
    def _():
        to = 0
        for piece in pieces:
            rows = piece.shape[0]
            block_ref[to : to + rows, :] = piece[...]
            to += rows

    if last:
        kept_ref, *by_x_refs, kept_y_ref, by_y_ref, total_ref = outs
    elif not first:
        (total_ref,) = outs
    else:
        total_ref, lam_ref = outs
        for k in range(NX):

            @pl.when(g == k)
            def _():
                lam_ref[...] = lam_refs[k][...]

    lam = lam_ref[...]
    part = lam.shape[0] // 2
    rows = block_ref.shape[0]
    for at in range(0, rows, chunk):
        size = min(chunk, rows - at)
        block = block_ref[at : at + size, :]
        weighted = lax.dot_general(
            lam, block, (((1,), (1,)), ((), ())), preferred_element_type=jnp.float32
        )
        divided = []
        for k in range(2):
            denom = base_ref[k : k + 1, at : at + size] - ea_ref[k * part : (k + 1) * part, :]
            inverse = pl.reciprocal(denom, approx=True)
            inverse = inverse * (2.0 - denom * inverse)
            divided.append(weighted[k * part : (k + 1) * part] * inverse)
        triples = jnp.concatenate(divided, axis=0).astype(jnp.bfloat16)
        share = jnp.dot(triples, block, preferred_element_type=jnp.float32)
        if at:
            total_ref[...] += share
        elif first:
            total_ref[...] = share
        else:
            total_ref[...] = prev_ref[...] + share
    if not last:
        return
    wide = by_y_ref.shape[2]
    mid = part + part // 2

    @pl.when(g == 0)
    def _():
        kept_ref[...] = total_ref[:part, :]

    for k in range(1, NX):

        @pl.when(g == k)
        def _():
            by_x_refs[k - 1][...] = encode(total_ref[:part, :], wide)

    kept_y_ref[0] = total_ref[part:mid, :]
    by_y_ref[0] = encode(total_ref[mid:, :], wide)


def whole(shape):
    return pl.BlockSpec(shape, lambda g: (0,) * len(shape))


def by_step(shape):
    return pl.BlockSpec((1,) + shape[1:], lambda g: (g, 0, 0))


def triples_call(base, ea, lams, prev, pieces, last=False):
    first = prev is None
    rows = sum(p.shape[0] for p in pieces)
    tile, width = lams[0].shape if first else (lams.shape[0] // NX, lams.shape[1])
    padded = -(-rows // 128) * 128
    base = jnp.pad(base, ((0, 0), (0, padded - rows)), constant_values=1.0)
    spec = pl.BlockSpec((tile, width), lambda g: (g, 0))
    in_specs = [whole(base.shape), pl.BlockSpec((tile, 1), lambda g: (g, 0))]
    in_specs += [whole(p.shape) for p in lams] if first else [spec, spec]
    in_specs += [whole(p.shape) for p in pieces]
    args = [base, ea, *(lams if first else [lams, prev]), *pieces]
    scratch = [pltpu.VMEM((rows, width), jnp.bfloat16)]
    if last:
        half = tile // 2
        wide = -(-(width + 1) // 128) * 128
        shapes = [((half, width), jnp.float32)] + [((half, wide), jnp.int16)] * (NX - 1)
        out_specs = [whole(shape) for shape, _ in shapes]
        pair = [((NX, half // 2, width), jnp.float32), ((NX, half // 2, wide), jnp.int16)]
        out_specs += [by_step(shape) for shape, _ in pair]
        shapes += pair
        scratch = [pltpu.VMEM((tile, width), jnp.float32)] + scratch
    else:
        shapes = [((NX * tile, width), jnp.float32), ((NX * tile, width), jnp.bfloat16)]
        shapes = shapes[: 1 + first]
        out_specs = [spec] * len(shapes)
    return pl.pallas_call(
        functools.partial(triples_kernel, len(pieces), first, last, 512),
        grid=(NX,),
        in_specs=in_specs,
        out_specs=out_specs,
        out_shape=[jax.ShapeDtypeStruct(*shape) for shape in shapes],
        scratch_shapes=scratch,
        compiler_params=pltpu.CompilerParams(vmem_limit_bytes=40 * 1024 * 1024),
        cost_estimate=pl.CostEstimate(
            flops=4 * rows * NX * tile * width,
            bytes_accessed=2 * rows * width + 10 * NX * tile * width,
            transcendentals=0,
        ),
    )(*args)


def recode_kernel(kept_ref, got_ref, own_ref, *coded_refs):
    g = pl.program_id(0)
    total = kept_ref[0] + decode(got_ref[0], kept_ref.shape[2])

    @pl.when(g == 0)
    def _():
        own_ref[...] = total

    for k in range(1, NX):

        @pl.when(g == k)
        def _():
            coded_refs[k - 1][...] = encode(total, got_ref.shape[2])


def recode(kept, got):
    shapes = [(kept.shape[1:], jnp.float32)] + [(got.shape[1:], jnp.int16)] * (NX - 1)
    return pl.pallas_call(
        recode_kernel,
        grid=(NX,),
        in_specs=[by_step(kept.shape), by_step(got.shape)],
        out_specs=[whole(shape) for shape, _ in shapes],
        out_shape=[jax.ShapeDtypeStruct(*shape) for shape in shapes],
        compiler_params=pltpu.CompilerParams(vmem_limit_bytes=16 * 1024 * 1024),
        cost_estimate=pl.CostEstimate(
            flops=10 * kept.size, bytes_accessed=10 * kept.size, transcendentals=0
        ),
    )(kept, got)


def body(lambda_pairs, vvvo, pair_list, owned_occ, step_root, occ_energy, virt_energy):
    window, local_b, width = vvvo.shape
    n_rows = window * local_b
    batch_pos = lax.axis_index("batch")
    slab_pos = lax.axis_index("slab")
    core = batch_pos % NC
    yh = (batch_pos // NC) % NYH
    z = batch_pos // (NC * NYH)
    x = slab_pos // NYL
    yl = slab_pos % NYL
    up = core == 0
    ahead_sign = 1 - 2 * core
    root_own = jnp.where(up, step_root[0], step_root[1])
    root_other = jnp.where(up, step_root[1], step_root[0])

    pair_list_other = send(pair_list, SWAP_CORE)

    own = lax.dynamic_index_in_dim(lambda_pairs, core, 0, keepdims=False)
    give = lax.dynamic_index_in_dim(lambda_pairs, 1 - core, 0, keepdims=False)
    lam_pair = jnp.stack([own, send(give, SWAP_CORE)])
    lam = jnp.stack([lam_pair, send(lam_pair, SWAP_YL)], axis=1).reshape(2 * NYL * local_b, width)

    piece = -(-n_rows // (NZ * 16)) * 16

    flat = vvvo.transpose(1, 0, 2).reshape(n_rows, width)
    far = NZ // 2

    def ahead(sign, steps):
        start = jnp.minimum((z + sign * steps) % NZ * piece, n_rows - piece)
        return lax.dynamic_slice_in_dim(flat, start, piece)

    swapped = {k: send(ahead(-ahead_sign, k), SWAP_CORE) for k in range(far, -1, -1)}

    def inject(root, steps, theirs):
        return jnp.where(root % NC == core, ahead(ahead_sign, steps), theirs)

    def on_root(root):
        return root // NC == batch_pos // NC

    def after(array, earlier):
        return lax.optimization_barrier((array, earlier))[0]

    def both(*arrays):
        return lax.optimization_barrier(arrays)

    give_own = inject(root_own, far, swapped[far])
    got_own = send(give_own, Z_RING)
    give_other = got_other = None
    for k in range(far - 1, 0, -1):
        if give_other is not None:
            got_own = after(got_own, give_other)
        if k == far - 1:
            got_own, lam_pair = both(got_own, lam_pair)
        elif k == far - 2:
            got_own, lam = both(got_own, lam)
            lam_x = {step: send(lam, x_by(-step)) for step in (1, NX - 1, 2)}
        elif k == far - 3:
            got_own, lam_x[1], lam_x[NX - 1] = both(got_own, lam_x[1], lam_x[NX - 1])
        give_own = jnp.where(on_root(root_own), inject(root_own, k, swapped[k]), got_own)
        got_own = send(give_own, Z_RING)
        if got_other is None:
            give_other = inject(root_other, k, after(swapped[k], give_own))
        else:
            got_other = after(got_other, give_own)
            give_other = jnp.where(
                on_root(root_other), inject(root_other, k, swapped[k]), got_other
            )
        got_other = send(give_other, Z_RING)
    got_own, lam_x[2] = both(got_own, lam_x[2])
    crossed = send(got_other, SWAP_CORE)
    along = ((z - root_own // (NC * NYH)) * ahead_sign) % NZ
    mine = jnp.where(
        on_root(root_own),
        inject(root_own, 0, swapped[0]),
        jnp.where(along <= far, got_own, crossed),
    )
    occ_energy, virt_energy, _ = both(occ_energy, virt_energy, mine)
    pairs = jnp.concatenate(
        [lax.dynamic_index_in_dim(p, core, 0) for p in (pair_list, pair_list_other)]
    )
    occ_sum = occ_energy[pairs[:, 0]] + occ_energy[pairs[:, 1]] + occ_energy[owned_occ[root_own]]
    energy_b = lax.dynamic_slice_in_dim(virt_energy, slab_pos * local_b, local_b)
    energy_c = virt_energy[:window]
    base = ((occ_sum[:, None, None] - energy_c) - energy_b[:, None]).reshape(2, n_rows)
    last = (NZ - 1) * piece
    spare = NZ * piece - n_rows
    base = jnp.concatenate(
        [base[:, :last], jnp.full((2, spare), 1e30, jnp.float32), base[:, last:]], axis=1
    ).reshape(2, NZ, piece)
    base = lax.dynamic_slice_in_dim(jnp.concatenate([base, base], axis=1), z, NZ, axis=1)
    base = jnp.where(up, jnp.roll(base[:, ::-1], 1, axis=1), base)
    ea = virt_energy.reshape(NX, NYL, local_b)
    ea = jnp.where(yl == 0, ea, ea[:, ::-1])
    ea = lax.dynamic_slice_in_dim(jnp.concatenate([ea, ea], axis=0), x, NX, axis=0)
    ea = jnp.stack([ea, ea], axis=1).reshape(NX * 2 * NYL * local_b, 1)

    here = jnp.where((root_own // NC) % NYH == yh, mine, send(mine, SWAP_YH))
    lams = [lam, lam_x[1], lam_x[2], lam_x[NX - 1]]

    def base_of(order):
        return jnp.concatenate([base[:, k] for k in order], axis=1)

    here, base, ea, *lams = both(here, base, ea, *lams)
    ring_own, ring_other, crossed = [here], [send(here, SWAP_CORE)], [here]
    for k in range(1, far):
        if k == far - 1:
            ring_other[-1] = after(ring_other[-1], total)
        ring_own.append(send(ring_own[-1], Z_RING))
        ring_other.append(send(ring_other[-1], Z_RING))
        crossed.append(send(ring_other[-1], SWAP_CORE))
        if k == 1:
            early = [here, ring_own[1], crossed[1]]
            total, lam = triples_call(base_of([0, 1, 7]), ea, lams, None, early)
    farthest = send(ring_own[-1], Z_RING)
    (total,) = triples_call(base_of([2, 6]), ea, lam, total, [ring_own[2], crossed[2]])
    late = [ring_own[3], crossed[3], farthest]
    kept, *by_x, kept_y, by_y = triples_call(base_of([3, 5, 4]), ea, lam, total, late, last=True)

    got_y = send(by_y, SWAP_YL)
    got_x = [send(by_x[step - 1], x_by(step)) for step in (2, 1, 3)]
    other, *coded = recode(kept_y, got_y)
    own = kept + sum(decode(got, width) for got in got_x)
    own = own[:local_b] + send(own[local_b:], SWAP_YL)
    got_x = [send(coded[step - 1], x_by(step)) for step in (2, 1, 3)]
    other = send(other + sum(decode(got, width) for got in got_x), SWAP_CORE)
    return jnp.where(up, jnp.stack([own, other]), jnp.stack([other, own]))


def solution(mesh):
    placed = (
        P("batch", "slab", None),
        P("batch", "slab", None),
        P("batch", None),
        P(),
        P(),
        P(),
        P(),
    )
    return jax.shard_map(
        body, mesh=mesh, in_specs=placed, out_specs=P("batch", "slab", None), check_vma=False
    )
```

```python
import functools

import jax
import jax.numpy as jnp
from jax import lax
from jax.experimental import pallas as pl
from jax.experimental.pallas import tpu as pltpu
from jax.sharding import PartitionSpec as P

AXES = ("batch", "slab")
NZ, NYH, NC, NX, NYL = 8, 2, 2, 4, 2


def full_perm(move):
    pairs = []
    for device in range(NZ * NYH * NC * NX * NYL):
        rest, yl = divmod(device, NYL)
        rest, x = divmod(rest, NX)
        rest, core = divmod(rest, NC)
        z, yh = divmod(rest, NYH)
        z, yh, core, x, yl = move(z, yh, core, x, yl)
        target = (((z % NZ) * NYH + yh % NYH) * NC + core % NC) * NX + x % NX
        pairs.append((device, target * NYL + yl % NYL))
    return pairs


SWAP_CORE = full_perm(lambda z, h, c, x, l: (z, h, 1 - c, x, l))
SWAP_YH = full_perm(lambda z, h, c, x, l: (z, 1 - h, c, x, l))
SWAP_YL = full_perm(lambda z, h, c, x, l: (z, h, c, x, 1 - l))
Z_RING = full_perm(lambda z, h, c, x, l: (z + 1 - 2 * c, h, c, x, l))


def x_by(step):
    return full_perm(lambda z, h, c, x, l: (z, h, c, x + step, l))


def send(array, perm):
    return lax.ppermute(array, AXES, perm)


def encode(value, wide):
    top = jnp.maximum(jnp.max(jnp.abs(value), axis=1, keepdims=True), 2.0**-110)
    exponent = jnp.ceil(jnp.log(top * 1.0001) * 1.4426950408889634) - 15.0
    coded = jnp.floor(value * jnp.exp2(-exponent) + 0.5)
    tail = jnp.broadcast_to(exponent, (value.shape[0], wide - value.shape[1]))
    return jnp.concatenate([coded, tail], axis=1).astype(jnp.int32).astype(jnp.int16)


def decode(coded, width):
    coded = coded.astype(jnp.float32)
    return coded[:, :width] * jnp.exp2(coded[:, width : width + 1])


def triples_kernel(n_pieces, first, last, chunk, *refs):
    base_ref, ea_ref = refs[:2]
    if first:
        lam_refs = refs[2 : 2 + NX]
        at = 2 + NX
    else:
        lam_ref, prev_ref = refs[2:4]
        at = 4
    pieces = refs[at : at + n_pieces]
    outs = refs[at + n_pieces : len(refs) - 1]
    block_ref = refs[-1]
    g = pl.program_id(0)

    @pl.when(g == 0)
    def _():
        to = 0
        for piece in pieces:
            rows = piece.shape[0]
            block_ref[to : to + rows, :] = piece[...]
            to += rows

    if last:
        kept_ref, *by_x_refs, kept_y_ref, by_y_ref, total_ref = outs
    elif not first:
        (total_ref,) = outs
    else:
        total_ref, lam_ref = outs
        for k in range(NX):

            @pl.when(g == k)
            def _():
                lam_ref[...] = lam_refs[k][...]

    lam = lam_ref[...]
    part = lam.shape[0] // 2
    rows = block_ref.shape[0]
    for at in range(0, rows, chunk):
        size = min(chunk, rows - at)
        block = block_ref[at : at + size, :]
        weighted = lax.dot_general(
            lam, block, (((1,), (1,)), ((), ())), preferred_element_type=jnp.float32
        )
        divided = []
        for k in range(2):
            denom = base_ref[k : k + 1, at : at + size] - ea_ref[k * part : (k + 1) * part, :]
            inverse = pl.reciprocal(denom, approx=True)
            inverse = inverse * (2.0 - denom * inverse)
            divided.append(weighted[k * part : (k + 1) * part] * inverse)
        triples = jnp.concatenate(divided, axis=0).astype(jnp.bfloat16)
        share = jnp.dot(triples, block, preferred_element_type=jnp.float32)
        if at:
            total_ref[...] += share
        elif first:
            total_ref[...] = share
        else:
            total_ref[...] = prev_ref[...] + share
    if not last:
        return
    wide = by_y_ref.shape[2]
    mid = part + part // 2

    @pl.when(g == 0)
    def _():
        kept_ref[...] = total_ref[:part, :]

    for k in range(1, NX):

        @pl.when(g == k)
        def _():
            by_x_refs[k - 1][...] = encode(total_ref[:part, :], wide)

    kept_y_ref[0] = total_ref[part:mid, :]
    by_y_ref[0] = encode(total_ref[mid:, :], wide)


def whole(shape):
    return pl.BlockSpec(shape, lambda g: (0,) * len(shape))


def held(shape):
    return pl.BlockSpec(shape, lambda g: (0,) * len(shape), pipeline_mode=pl.Buffered(1))


def by_step(shape):
    return pl.BlockSpec((1,) + shape[1:], lambda g: (g, 0, 0))


def triples_call(base, ea, lams, prev, pieces, last=False):
    first = prev is None
    rows = sum(p.shape[0] for p in pieces)
    tile, width = lams[0].shape if first else (lams.shape[0] // NX, lams.shape[1])
    padded = -(-rows // 128) * 128
    base = jnp.pad(base, ((0, 0), (0, padded - rows)), constant_values=1.0)
    spec = pl.BlockSpec((tile, width), lambda g: (g, 0))
    in_specs = [held(base.shape), pl.BlockSpec((tile, 1), lambda g: (g, 0))]
    in_specs += [held(p.shape) for p in lams] if first else [spec, spec]
    in_specs += [held(p.shape) for p in pieces]
    args = [base, ea, *(lams if first else [lams, prev]), *pieces]
    scratch = [pltpu.VMEM((rows, width), jnp.bfloat16)]
    if last:
        half = tile // 2
        wide = -(-(width + 1) // 128) * 128
        shapes = [((half, width), jnp.float32)] + [((half, wide), jnp.int16)] * (NX - 1)
        out_specs = [whole(shape) for shape, _ in shapes]
        pair = [((NX, half // 2, width), jnp.float32), ((NX, half // 2, wide), jnp.int16)]
        out_specs += [by_step(shape) for shape, _ in pair]
        shapes += pair
        scratch = [pltpu.VMEM((tile, width), jnp.float32)] + scratch
    else:
        shapes = [((NX * tile, width), jnp.float32), ((NX * tile, width), jnp.bfloat16)]
        shapes = shapes[: 1 + first]
        out_specs = [spec] * len(shapes)
    return pl.pallas_call(
        functools.partial(triples_kernel, len(pieces), first, last, 512),
        grid=(NX,),
        in_specs=in_specs,
        out_specs=out_specs,
        out_shape=[jax.ShapeDtypeStruct(*shape) for shape in shapes],
        scratch_shapes=scratch,
        compiler_params=pltpu.CompilerParams(vmem_limit_bytes=24 * 1024 * 1024),
        cost_estimate=pl.CostEstimate(
            flops=4 * rows * NX * tile * width,
            bytes_accessed=2 * rows * width + 10 * NX * tile * width,
            transcendentals=0,
        ),
    )(*args)


def recode_kernel(kept_ref, got_ref, own_ref, *coded_refs):
    g = pl.program_id(0)
    total = kept_ref[0] + decode(got_ref[0], kept_ref.shape[2])

    @pl.when(g == 0)
    def _():
        own_ref[...] = total

    for k in range(1, NX):

        @pl.when(g == k)
        def _():
            coded_refs[k - 1][...] = encode(total, got_ref.shape[2])


def recode(kept, got):
    shapes = [(kept.shape[1:], jnp.float32)] + [(got.shape[1:], jnp.int16)] * (NX - 1)
    return pl.pallas_call(
        recode_kernel,
        grid=(NX,),
        in_specs=[by_step(kept.shape), by_step(got.shape)],
        out_specs=[whole(shape) for shape, _ in shapes],
        out_shape=[jax.ShapeDtypeStruct(*shape) for shape in shapes],
        compiler_params=pltpu.CompilerParams(vmem_limit_bytes=16 * 1024 * 1024),
        cost_estimate=pl.CostEstimate(
            flops=10 * kept.size, bytes_accessed=10 * kept.size, transcendentals=0
        ),
    )(kept, got)


def body(lambda_pairs, vvvo, pair_list, owned_occ, step_root, occ_energy, virt_energy):
    window, local_b, width = vvvo.shape
    n_rows = window * local_b
    batch_pos = lax.axis_index("batch")
    slab_pos = lax.axis_index("slab")
    core = batch_pos % NC
    yh = (batch_pos // NC) % NYH
    z = batch_pos // (NC * NYH)
    x = slab_pos // NYL
    yl = slab_pos % NYL
    up = core == 0
    ahead_sign = 1 - 2 * core
    root_own = jnp.where(up, step_root[0], step_root[1])
    root_other = jnp.where(up, step_root[1], step_root[0])

    pair_list_other = send(pair_list, SWAP_CORE)

    own = lax.dynamic_index_in_dim(lambda_pairs, core, 0, keepdims=False)
    give = lax.dynamic_index_in_dim(lambda_pairs, 1 - core, 0, keepdims=False)
    lam_pair = jnp.stack([own, send(give, SWAP_CORE)])

    piece = -(-n_rows // (NZ * 16)) * 16

    flat = vvvo.transpose(1, 0, 2).reshape(n_rows, width)
    far = NZ // 2

    def ahead(sign, steps):
        start = jnp.minimum((z + sign * steps) % NZ * piece, n_rows - piece)
        return lax.dynamic_slice_in_dim(flat, start, piece)

    swapped = {k: send(ahead(-ahead_sign, k), SWAP_CORE) for k in range(far, -1, -1)}

    def inject(root, steps, theirs):
        return jnp.where(root % NC == core, ahead(ahead_sign, steps), theirs)

    def on_root(root):
        return root // NC == batch_pos // NC

    def after(array, earlier):
        return lax.optimization_barrier((array, earlier))[0]

    def both(*arrays):
        return lax.optimization_barrier(arrays)

    *early, lam_pair = both(*[swapped[k] for k in range(far, 0, -1)], lam_pair)
    swapped.update(zip(range(far, 0, -1), early))
    lam = jnp.stack([lam_pair, send(lam_pair, SWAP_YL)], axis=1).reshape(2 * NYL * local_b, width)
    give_own = inject(root_own, far, swapped[far])
    got_own = send(give_own, Z_RING)
    give_other = got_other = None
    for k in range(far - 1, 0, -1):
        if give_other is not None:
            got_own = after(got_own, give_other)
        if k == far - 1:
            got_own, lam = both(got_own, lam)
            lam_x = {step: send(lam, x_by(-step)) for step in (1, NX - 1, 2)}
        elif k == far - 2:
            got_other, lam_x[1], lam_x[NX - 1] = both(got_other, lam_x[1], lam_x[NX - 1])
        elif k == far - 3:
            got_other, lam_x[2] = both(got_other, lam_x[2])
        give_own = jnp.where(on_root(root_own), inject(root_own, k, swapped[k]), got_own)
        got_own = send(give_own, Z_RING)
        if got_other is None:
            give_other = inject(root_other, k, after(swapped[k], give_own))
        else:
            got_other = after(got_other, give_own)
            give_other = jnp.where(
                on_root(root_other), inject(root_other, k, swapped[k]), got_other
            )
        got_other = send(give_other, Z_RING)
    crossed = send(got_other, SWAP_CORE)
    along = ((z - root_own // (NC * NYH)) * ahead_sign) % NZ
    mine = jnp.where(
        on_root(root_own),
        inject(root_own, 0, swapped[0]),
        jnp.where(along <= far, got_own, crossed),
    )
    here = jnp.where((root_own // NC) % NYH == yh, mine, send(mine, SWAP_YH))
    lams = [lam, lam_x[1], lam_x[2], lam_x[NX - 1]]

    def base_of(order):
        return jnp.concatenate([base[:, k] for k in order], axis=1)

    here, *lams = both(here, *lams)
    ring_own, ring_other, crossed = [here], [send(here, SWAP_CORE)], [here]

    occ_energy, virt_energy, _ = both(occ_energy, virt_energy, ring_other[0])
    pairs = jnp.concatenate(
        [lax.dynamic_index_in_dim(p, core, 0) for p in (pair_list, pair_list_other)]
    )
    occ_sum = occ_energy[pairs[:, 0]] + occ_energy[pairs[:, 1]] + occ_energy[owned_occ[root_own]]
    energy_b = lax.dynamic_slice_in_dim(virt_energy, slab_pos * local_b, local_b)
    energy_c = virt_energy[:window]
    base = ((occ_sum[:, None, None] - energy_c) - energy_b[:, None]).reshape(2, n_rows)
    last = (NZ - 1) * piece
    spare = NZ * piece - n_rows
    base = jnp.concatenate(
        [base[:, :last], jnp.full((2, spare), 1e30, jnp.float32), base[:, last:]], axis=1
    ).reshape(2, NZ, piece)
    base = lax.dynamic_slice_in_dim(jnp.concatenate([base, base], axis=1), z, NZ, axis=1)
    base = jnp.where(up, jnp.roll(base[:, ::-1], 1, axis=1), base)
    ea = virt_energy.reshape(NX, NYL, local_b)
    ea = jnp.where(yl == 0, ea, ea[:, ::-1])
    ea = lax.dynamic_slice_in_dim(jnp.concatenate([ea, ea], axis=0), x, NX, axis=0)
    ea = jnp.stack([ea, ea], axis=1).reshape(NX * 2 * NYL * local_b, 1)

    for k in range(1, far):
        if k == far - 1:
            ring_own[-1], ring_other[-1], total = both(ring_own[-1], ring_other[-1], total)
        ring_own.append(send(ring_own[-1], Z_RING))
        ring_other.append(send(ring_other[-1], Z_RING))
        crossed.append(send(ring_other[-1], SWAP_CORE))
        if k == 1:
            early = [here, ring_own[1], crossed[1]]
            total, lam = triples_call(base_of([0, 1, 7]), ea, lams, None, early)
    farthest = send(ring_own[-1], Z_RING)
    middle = [after(ring_own[2], ring_own[3]), crossed[2]]
    (total,) = triples_call(base_of([2, 6]), ea, lam, total, middle)
    late = [ring_own[3], crossed[3], farthest]
    kept, *by_x, kept_y, by_y = triples_call(base_of([3, 5, 4]), ea, lam, total, late, last=True)

    got_y = send(by_y, SWAP_YL)
    got_x = [send(by_x[step - 1], x_by(step)) for step in (2, 1, 3)]
    other, *coded = recode(kept_y, got_y)
    own = kept + sum(decode(got, width) for got in got_x)
    own = own[:local_b] + send(own[local_b:], SWAP_YL)
    got_x = [send(coded[step - 1], x_by(step)) for step in (2, 1, 3)]
    other = send(other + sum(decode(got, width) for got in got_x), SWAP_CORE)
    return jnp.where(up, jnp.stack([own, other]), jnp.stack([other, own]))


def solution(mesh):
    placed = (
        P("batch", "slab", None),
        P("batch", "slab", None),
        P("batch", None),
        P(),
        P(),
        P(),
        P(),
    )
    return jax.shard_map(
        body, mesh=mesh, in_specs=placed, out_specs=P("batch", "slab", None), check_vma=False
    )
```

```python
import functools

import jax
import jax.numpy as jnp
from jax import lax
from jax.experimental import pallas as pl
from jax.experimental.pallas import tpu as pltpu
from jax.sharding import PartitionSpec as P

AXES = ("batch", "slab")
NZ, NYH, NC, NX, NYL = 8, 2, 2, 4, 2


def full_perm(move):
    pairs = []
    for device in range(NZ * NYH * NC * NX * NYL):
        rest, yl = divmod(device, NYL)
        rest, x = divmod(rest, NX)
        rest, core = divmod(rest, NC)
        z, yh = divmod(rest, NYH)
        z, yh, core, x, yl = move(z, yh, core, x, yl)
        target = (((z % NZ) * NYH + yh % NYH) * NC + core % NC) * NX + x % NX
        pairs.append((device, target * NYL + yl % NYL))
    return pairs


SWAP_CORE = full_perm(lambda z, h, c, x, l: (z, h, 1 - c, x, l))
SWAP_YH = full_perm(lambda z, h, c, x, l: (z, 1 - h, c, x, l))
SWAP_YL = full_perm(lambda z, h, c, x, l: (z, h, c, x, 1 - l))
Z_RING = full_perm(lambda z, h, c, x, l: (z + 1 - 2 * c, h, c, x, l))


def x_by(step):
    return full_perm(lambda z, h, c, x, l: (z, h, c, x + step, l))


def send(array, perm):
    return lax.ppermute(array, AXES, perm)


def encode(value, wide):
    top = jnp.maximum(jnp.max(jnp.abs(value), axis=1, keepdims=True), 2.0**-110)
    exponent = jnp.ceil(jnp.log(top * 1.0001) * 1.4426950408889634) - 15.0
    coded = jnp.floor(value * jnp.exp2(-exponent) + 0.5)
    tail = jnp.broadcast_to(exponent, (value.shape[0], wide - value.shape[1]))
    return jnp.concatenate([coded, tail], axis=1).astype(jnp.int32).astype(jnp.int16)


def decode(coded, width):
    coded = coded.astype(jnp.float32)
    return coded[:, :width] * jnp.exp2(coded[:, width : width + 1])


def triples_kernel(n_pieces, first, last, chunk, *refs):
    base_ref, ea_ref = refs[:2]
    if first:
        lam_refs = refs[2 : 2 + NX]
        at = 2 + NX
    else:
        lam_ref, prev_ref = refs[2:4]
        at = 4
    pieces = refs[at : at + n_pieces]
    outs = refs[at + n_pieces : len(refs) - 1]
    block_ref = refs[-1]
    g = pl.program_id(0)

    @pl.when(g == 0)
    def _():
        to = 0
        for piece in pieces:
            rows = piece.shape[0]
            block_ref[to : to + rows, :] = piece[...]
            to += rows

    if last:
        kept_ref, *by_x_refs, kept_y_ref, by_y_ref, total_ref = outs
    elif not first:
        (total_ref,) = outs
    else:
        total_ref, lam_ref = outs
        for k in range(NX):

            @pl.when(g == k)
            def _():
                lam_ref[...] = lam_refs[k][...]

    lam = lam_ref[...]
    part = lam.shape[0] // 2
    rows = block_ref.shape[0]
    for at in range(0, rows, chunk):
        size = min(chunk, rows - at)
        block = block_ref[at : at + size, :]
        weighted = lax.dot_general(
            lam, block, (((1,), (1,)), ((), ())), preferred_element_type=jnp.float32
        )
        divided = []
        for k in range(2):
            denom = base_ref[k : k + 1, at : at + size] - ea_ref[k * part : (k + 1) * part, :]
            inverse = pl.reciprocal(denom, approx=True)
            inverse = inverse * (2.0 - denom * inverse)
            divided.append(weighted[k * part : (k + 1) * part] * inverse)
        triples = jnp.concatenate(divided, axis=0).astype(jnp.bfloat16)
        share = jnp.dot(triples, block, preferred_element_type=jnp.float32)
        if at:
            total_ref[...] += share
        elif first:
            total_ref[...] = share
        else:
            total_ref[...] = prev_ref[...] + share
    if not last:
        return
    wide = by_y_ref.shape[2]
    mid = part + part // 2

    @pl.when(g == 0)
    def _():
        kept_ref[...] = total_ref[:part, :]

    for k in range(1, NX):

        @pl.when(g == k)
        def _():
            by_x_refs[k - 1][...] = encode(total_ref[:part, :], wide)

    kept_y_ref[0] = total_ref[part:mid, :]
    by_y_ref[0] = encode(total_ref[mid:, :], wide)


def whole(shape):
    return pl.BlockSpec(shape, lambda g: (0,) * len(shape))


def held(shape):
    return pl.BlockSpec(shape, lambda g: (0,) * len(shape), pipeline_mode=pl.Buffered(1))


def by_step(shape):
    return pl.BlockSpec((1,) + shape[1:], lambda g: (g, 0, 0))


def triples_call(base, ea, lams, prev, pieces, last=False):
    first = prev is None
    rows = sum(p.shape[0] for p in pieces)
    tile, width = lams[0].shape if first else (lams.shape[0] // NX, lams.shape[1])
    padded = -(-rows // 128) * 128
    base = jnp.pad(base, ((0, 0), (0, padded - rows)), constant_values=1.0)
    spec = pl.BlockSpec((tile, width), lambda g: (g, 0))
    in_specs = [held(base.shape), pl.BlockSpec((tile, 1), lambda g: (g, 0))]
    in_specs += [held(p.shape) for p in lams] if first else [spec, spec]
    in_specs += [held(p.shape) for p in pieces]
    args = [base, ea, *(lams if first else [lams, prev]), *pieces]
    scratch = [pltpu.VMEM((rows, width), jnp.bfloat16)]
    if last:
        half = tile // 2
        wide = -(-(width + 1) // 128) * 128
        shapes = [((half, width), jnp.float32)] + [((half, wide), jnp.int16)] * (NX - 1)
        out_specs = [whole(shape) for shape, _ in shapes]
        pair = [((NX, half // 2, width), jnp.float32), ((NX, half // 2, wide), jnp.int16)]
        out_specs += [by_step(shape) for shape, _ in pair]
        shapes += pair
        scratch = [pltpu.VMEM((tile, width), jnp.float32)] + scratch
    else:
        shapes = [((NX * tile, width), jnp.float32), ((NX * tile, width), jnp.bfloat16)]
        shapes = shapes[: 1 + first]
        out_specs = [spec] * len(shapes)
    return pl.pallas_call(
        functools.partial(triples_kernel, len(pieces), first, last, 512),
        grid=(NX,),
        in_specs=in_specs,
        out_specs=out_specs,
        out_shape=[jax.ShapeDtypeStruct(*shape) for shape in shapes],
        scratch_shapes=scratch,
        compiler_params=pltpu.CompilerParams(vmem_limit_bytes=24 * 1024 * 1024),
        cost_estimate=pl.CostEstimate(
            flops=4 * rows * NX * tile * width,
            bytes_accessed=2 * rows * width + 10 * NX * tile * width,
            transcendentals=0,
        ),
    )(*args)


def recode_kernel(kept_ref, got_ref, own_ref, *coded_refs):
    g = pl.program_id(0)
    total = kept_ref[0] + decode(got_ref[0], kept_ref.shape[2])

    @pl.when(g == 0)
    def _():
        own_ref[...] = total

    for k in range(1, NX):

        @pl.when(g == k)
        def _():
            coded_refs[k - 1][...] = encode(total, got_ref.shape[2])


def recode(kept, got):
    shapes = [(kept.shape[1:], jnp.float32)] + [(got.shape[1:], jnp.int16)] * (NX - 1)
    return pl.pallas_call(
        recode_kernel,
        grid=(NX,),
        in_specs=[by_step(kept.shape), by_step(got.shape)],
        out_specs=[whole(shape) for shape, _ in shapes],
        out_shape=[jax.ShapeDtypeStruct(*shape) for shape in shapes],
        compiler_params=pltpu.CompilerParams(vmem_limit_bytes=16 * 1024 * 1024),
        cost_estimate=pl.CostEstimate(
            flops=10 * kept.size, bytes_accessed=10 * kept.size, transcendentals=0
        ),
    )(kept, got)


def body(lambda_pairs, vvvo, pair_list, owned_occ, step_root, occ_energy, virt_energy):
    window, local_b, width = vvvo.shape
    n_rows = window * local_b
    batch_pos = lax.axis_index("batch")
    slab_pos = lax.axis_index("slab")
    core = batch_pos % NC
    yh = (batch_pos // NC) % NYH
    z = batch_pos // (NC * NYH)
    x = slab_pos // NYL
    yl = slab_pos % NYL
    up = core == 0
    ahead_sign = 1 - 2 * core
    root_own = jnp.where(up, step_root[0], step_root[1])
    root_other = jnp.where(up, step_root[1], step_root[0])

    pair_list_other = send(pair_list, SWAP_CORE)

    own = lax.dynamic_index_in_dim(lambda_pairs, core, 0, keepdims=False)
    give = lax.dynamic_index_in_dim(lambda_pairs, 1 - core, 0, keepdims=False)
    lam_pair = jnp.stack([own, send(give, SWAP_CORE)])

    piece = -(-n_rows // (NZ * 16)) * 16

    flat = vvvo.transpose(1, 0, 2).reshape(n_rows, width)
    far = NZ // 2

    def ahead(sign, steps):
        start = jnp.minimum((z + sign * steps) % NZ * piece, n_rows - piece)
        return lax.dynamic_slice_in_dim(flat, start, piece)

    swapped = {k: send(ahead(-ahead_sign, k), SWAP_CORE) for k in range(far, -1, -1)}

    def inject(root, steps, theirs):
        return jnp.where(root % NC == core, ahead(ahead_sign, steps), theirs)

    def on_root(root):
        return root // NC == batch_pos // NC

    def after(array, earlier):
        return lax.optimization_barrier((array, earlier))[0]

    def both(*arrays):
        return lax.optimization_barrier(arrays)

    *early, lam_pair = both(*[swapped[k] for k in range(far, 0, -1)], lam_pair)
    swapped.update(zip(range(far, 0, -1), early))
    lam = jnp.stack([lam_pair, send(lam_pair, SWAP_YL)], axis=1).reshape(2 * NYL * local_b, width)
    give_own = inject(root_own, far, swapped[far])

    occ_energy, virt_energy, _ = both(occ_energy, virt_energy, give_own)
    pairs = jnp.concatenate(
        [lax.dynamic_index_in_dim(p, core, 0) for p in (pair_list, pair_list_other)]
    )
    occ_sum = occ_energy[pairs[:, 0]] + occ_energy[pairs[:, 1]] + occ_energy[owned_occ[root_own]]
    energy_b = lax.dynamic_slice_in_dim(virt_energy, slab_pos * local_b, local_b)
    energy_c = virt_energy[:window]
    base = ((occ_sum[:, None, None] - energy_c) - energy_b[:, None]).reshape(2, n_rows)
    last = (NZ - 1) * piece
    spare = NZ * piece - n_rows
    base = jnp.concatenate(
        [base[:, :last], jnp.full((2, spare), 1e30, jnp.float32), base[:, last:]], axis=1
    ).reshape(2, NZ, piece)
    base = lax.dynamic_slice_in_dim(jnp.concatenate([base, base], axis=1), z, NZ, axis=1)
    base = jnp.where(up, jnp.roll(base[:, ::-1], 1, axis=1), base)
    ea = virt_energy.reshape(NX, NYL, local_b)
    ea = jnp.where(yl == 0, ea, ea[:, ::-1])
    ea = lax.dynamic_slice_in_dim(jnp.concatenate([ea, ea], axis=0), x, NX, axis=0)
    ea = jnp.stack([ea, ea], axis=1).reshape(NX * 2 * NYL * local_b, 1)

    got_own = send(give_own, Z_RING)
    give_other = got_other = None
    for k in range(far - 1, 0, -1):
        if give_other is not None:
            got_own = after(got_own, give_other)
        if k == far - 1:
            got_own, lam = both(got_own, lam)
            got_own, base, ea = both(got_own, base, ea)
        elif k == far - 2:
            lam_x = {step: send(after(lam, give_other), x_by(-step)) for step in (1, NX - 1)}
        elif k == far - 3:
            got_own, lam_x[1], lam_x[NX - 1] = both(got_own, lam_x[1], lam_x[NX - 1])
            lam_x[2] = send(after(lam, lam_x[1]), x_by(-2))
        give_own = jnp.where(on_root(root_own), inject(root_own, k, swapped[k]), got_own)
        got_own = send(give_own, Z_RING)
        if got_other is None:
            give_other = inject(root_other, k, after(swapped[k], give_own))
        else:
            got_other = after(got_other, give_own)
            give_other = jnp.where(
                on_root(root_other), inject(root_other, k, swapped[k]), got_other
            )
        got_other = send(give_other, Z_RING)
    crossed = send(got_other, SWAP_CORE)
    crossed, lam_x[2] = both(crossed, lam_x[2])
    along = ((z - root_own // (NC * NYH)) * ahead_sign) % NZ
    mine = jnp.where(
        on_root(root_own),
        inject(root_own, 0, swapped[0]),
        jnp.where(along <= far, got_own, crossed),
    )
    here = jnp.where((root_own // NC) % NYH == yh, mine, send(mine, SWAP_YH))
    lams = [lam, lam_x[1], lam_x[2], lam_x[NX - 1]]

    def base_of(order):
        return jnp.concatenate([base[:, k] for k in order], axis=1)

    here, *lams = both(here, *lams)
    ring_own, ring_other, crossed = [here], [send(here, SWAP_CORE)], [here]

    total, lam = triples_call(base_of([0]), ea, lams, None, [here])
    for k in range(1, far):
        if k == 2:
            ring_own[-1], total = both(ring_own[-1], total)
        ring_own.append(send(ring_own[-1], Z_RING))
        if k == 3:
            first = [after(ring_own[1], ring_own[2]), crossed[1]]
            (total,) = triples_call(base_of([1, 7]), ea, lam, total, first)
            ring_other[-1], total = both(ring_other[-1], total)
        ring_other.append(send(after(ring_other[-1], ring_own[k - 1]), Z_RING))
        crossed.append(send(ring_other[-1], SWAP_CORE))
    farthest = send(ring_own[-1], Z_RING)
    middle = [after(ring_own[2], ring_own[3]), crossed[2]]
    (total,) = triples_call(base_of([2, 6]), ea, lam, total, middle)
    late = [ring_own[3], crossed[3], farthest]
    kept, *by_x, kept_y, by_y = triples_call(base_of([3, 5, 4]), ea, lam, total, late, last=True)

    got_y = send(by_y, SWAP_YL)
    got_x = [send(by_x[step - 1], x_by(step)) for step in (2, 1, 3)]
    other, *coded = recode(kept_y, got_y)
    own = kept + sum(decode(got, width) for got in got_x)
    own = own[:local_b] + send(own[local_b:], SWAP_YL)
    got_x = [send(coded[step - 1], x_by(step)) for step in (2, 1, 3)]
    other = send(other + sum(decode(got, width) for got in got_x), SWAP_CORE)
    return jnp.where(up, jnp.stack([own, other]), jnp.stack([other, own]))


def solution(mesh):
    placed = (
        P("batch", "slab", None),
        P("batch", "slab", None),
        P("batch", None),
        P(),
        P(),
        P(),
        P(),
    )
    return jax.shard_map(
        body, mesh=mesh, in_specs=placed, out_specs=P("batch", "slab", None), check_vma=False
    )
```

```python
import functools

import jax
import jax.numpy as jnp
from jax import lax
from jax.experimental import pallas as pl
from jax.experimental.pallas import tpu as pltpu
from jax.sharding import PartitionSpec as P

AXES = ("batch", "slab")
NZ, NYH, NC, NX, NYL = 8, 2, 2, 4, 2


def full_perm(move):
    pairs = []
    for device in range(NZ * NYH * NC * NX * NYL):
        rest, yl = divmod(device, NYL)
        rest, x = divmod(rest, NX)
        rest, core = divmod(rest, NC)
        z, yh = divmod(rest, NYH)
        z, yh, core, x, yl = move(z, yh, core, x, yl)
        target = (((z % NZ) * NYH + yh % NYH) * NC + core % NC) * NX + x % NX
        pairs.append((device, target * NYL + yl % NYL))
    return pairs


SWAP_CORE = full_perm(lambda z, h, c, x, l: (z, h, 1 - c, x, l))
SWAP_YH = full_perm(lambda z, h, c, x, l: (z, 1 - h, c, x, l))
SWAP_YL = full_perm(lambda z, h, c, x, l: (z, h, c, x, 1 - l))
Z_RING = full_perm(lambda z, h, c, x, l: (z + 1 - 2 * c, h, c, x, l))


def x_by(step):
    return full_perm(lambda z, h, c, x, l: (z, h, c, x + step, l))


def send(array, perm):
    return lax.ppermute(array, AXES, perm)


def encode(value, wide):
    top = jnp.maximum(jnp.max(jnp.abs(value), axis=1, keepdims=True), 2.0**-110)
    exponent = jnp.ceil(jnp.log(top * 1.0001) * 1.4426950408889634) - 15.0
    coded = jnp.floor(value * jnp.exp2(-exponent) + 0.5)
    tail = jnp.broadcast_to(exponent, (value.shape[0], wide - value.shape[1]))
    return jnp.concatenate([coded, tail], axis=1).astype(jnp.int32).astype(jnp.int16)


def decode(coded, width):
    coded = coded.astype(jnp.float32)
    return coded[:, :width] * jnp.exp2(coded[:, width : width + 1])


def triples_kernel(n_pieces, first, last, chunk, *refs):
    base_ref, ea_ref = refs[:2]
    if first:
        lam_refs = refs[2 : 2 + NX]
        at = 2 + NX
    else:
        lam_ref, prev_ref = refs[2:4]
        at = 4
    pieces = refs[at : at + n_pieces]
    outs = refs[at + n_pieces : len(refs) - 1]
    block_ref = refs[-1]
    g = pl.program_id(0)

    @pl.when(g == 0)
    def _():
        to = 0
        for piece in pieces:
            rows = piece.shape[0]
            block_ref[to : to + rows, :] = piece[...]
            to += rows

    if last:
        kept_ref, *by_x_refs, kept_y_ref, by_y_ref, total_ref = outs
    elif not first:
        (total_ref,) = outs
    else:
        total_ref, lam_ref = outs
        for k in range(NX):

            @pl.when(g == k)
            def _():
                lam_ref[...] = lam_refs[k][...]

    lam = lam_ref[...]
    part = lam.shape[0] // 2
    rows = block_ref.shape[0]
    for at in range(0, rows, chunk):
        size = min(chunk, rows - at)
        block = block_ref[at : at + size, :]
        weighted = lax.dot_general(
            lam, block, (((1,), (1,)), ((), ())), preferred_element_type=jnp.float32
        )
        divided = []
        for k in range(2):
            denom = base_ref[k : k + 1, at : at + size] - ea_ref[k * part : (k + 1) * part, :]
            inverse = pl.reciprocal(denom, approx=True)
            inverse = inverse * (2.0 - denom * inverse)
            divided.append(weighted[k * part : (k + 1) * part] * inverse)
        triples = jnp.concatenate(divided, axis=0).astype(jnp.bfloat16)
        share = jnp.dot(triples, block, preferred_element_type=jnp.float32)
        if at:
            total_ref[...] += share
        elif first:
            total_ref[...] = share
        else:
            total_ref[...] = prev_ref[...] + share
    if not last:
        return
    wide = by_y_ref.shape[2]
    mid = part + part // 2

    @pl.when(g == 0)
    def _():
        kept_ref[...] = total_ref[:part, :]

    for k in range(1, NX):

        @pl.when(g == k)
        def _():
            by_x_refs[k - 1][...] = encode(total_ref[:part, :], wide)

    kept_y_ref[0] = total_ref[part:mid, :]
    by_y_ref[0] = encode(total_ref[mid:, :], wide)


def whole(shape):
    return pl.BlockSpec(shape, lambda g: (0,) * len(shape))


def held(shape):
    return pl.BlockSpec(shape, lambda g: (0,) * len(shape), pipeline_mode=pl.Buffered(1))


def by_step(shape):
    return pl.BlockSpec((1,) + shape[1:], lambda g: (g, 0, 0))


def triples_call(base, ea, lams, prev, pieces, last=False):
    first = prev is None
    rows = sum(p.shape[0] for p in pieces)
    tile, width = lams[0].shape if first else (lams.shape[0] // NX, lams.shape[1])
    padded = -(-rows // 128) * 128
    base = jnp.pad(base, ((0, 0), (0, padded - rows)), constant_values=1.0)
    spec = pl.BlockSpec((tile, width), lambda g: (g, 0))
    in_specs = [held(base.shape), pl.BlockSpec((tile, 1), lambda g: (g, 0))]
    in_specs += [held(p.shape) for p in lams] if first else [spec, spec]
    in_specs += [held(p.shape) for p in pieces]
    args = [base, ea, *(lams if first else [lams, prev]), *pieces]
    scratch = [pltpu.VMEM((rows, width), jnp.bfloat16)]
    if last:
        half = tile // 2
        wide = -(-(width + 1) // 128) * 128
        shapes = [((half, width), jnp.float32)] + [((half, wide), jnp.int16)] * (NX - 1)
        out_specs = [whole(shape) for shape, _ in shapes]
        pair = [((NX, half // 2, width), jnp.float32), ((NX, half // 2, wide), jnp.int16)]
        out_specs += [by_step(shape) for shape, _ in pair]
        shapes += pair
        scratch = [pltpu.VMEM((tile, width), jnp.float32)] + scratch
    else:
        shapes = [((NX * tile, width), jnp.float32), ((NX * tile, width), jnp.bfloat16)]
        shapes = shapes[: 1 + first]
        out_specs = [spec] * len(shapes)
    return pl.pallas_call(
        functools.partial(triples_kernel, len(pieces), first, last, 512),
        grid=(NX,),
        in_specs=in_specs,
        out_specs=out_specs,
        out_shape=[jax.ShapeDtypeStruct(*shape) for shape in shapes],
        scratch_shapes=scratch,
        compiler_params=pltpu.CompilerParams(vmem_limit_bytes=24 * 1024 * 1024),
        cost_estimate=pl.CostEstimate(
            flops=4 * rows * NX * tile * width,
            bytes_accessed=2 * rows * width + 10 * NX * tile * width,
            transcendentals=0,
        ),
    )(*args)


def recode_kernel(kept_ref, got_ref, own_ref, *coded_refs):
    g = pl.program_id(0)
    total = kept_ref[0] + decode(got_ref[0], kept_ref.shape[2])

    @pl.when(g == 0)
    def _():
        own_ref[...] = total

    for k in range(1, NX):

        @pl.when(g == k)
        def _():
            coded_refs[k - 1][...] = encode(total, got_ref.shape[2])


def recode(kept, got):
    shapes = [(kept.shape[1:], jnp.float32)] + [(got.shape[1:], jnp.int16)] * (NX - 1)
    return pl.pallas_call(
        recode_kernel,
        grid=(NX,),
        in_specs=[by_step(kept.shape), by_step(got.shape)],
        out_specs=[whole(shape) for shape, _ in shapes],
        out_shape=[jax.ShapeDtypeStruct(*shape) for shape in shapes],
        compiler_params=pltpu.CompilerParams(vmem_limit_bytes=16 * 1024 * 1024),
        cost_estimate=pl.CostEstimate(
            flops=10 * kept.size, bytes_accessed=10 * kept.size, transcendentals=0
        ),
    )(kept, got)


def body(lambda_pairs, vvvo, pair_list, owned_occ, step_root, occ_energy, virt_energy):
    window, local_b, width = vvvo.shape
    n_rows = window * local_b
    batch_pos = lax.axis_index("batch")
    slab_pos = lax.axis_index("slab")
    core = batch_pos % NC
    yh = (batch_pos // NC) % NYH
    z = batch_pos // (NC * NYH)
    x = slab_pos // NYL
    yl = slab_pos % NYL
    up = core == 0
    ahead_sign = 1 - 2 * core
    root_own = jnp.where(up, step_root[0], step_root[1])
    root_other = jnp.where(up, step_root[1], step_root[0])

    pair_list_other = send(pair_list, SWAP_CORE)

    own = lax.dynamic_index_in_dim(lambda_pairs, core, 0, keepdims=False)
    give = lax.dynamic_index_in_dim(lambda_pairs, 1 - core, 0, keepdims=False)
    lam_got = send(give, SWAP_CORE)

    piece = -(-n_rows // (NZ * 16)) * 16

    flat = lax.optimization_barrier((vvvo, give))[0].transpose(1, 0, 2).reshape(n_rows, width)
    far = NZ // 2

    def ahead(sign, steps):
        start = jnp.minimum((z + sign * steps) % NZ * piece, n_rows - piece)
        return lax.dynamic_slice_in_dim(flat, start, piece)

    swapped = {k: send(ahead(-ahead_sign, k), SWAP_CORE) for k in range(far, -1, -1)}

    def inject(root, steps, theirs):
        return jnp.where(root % NC == core, ahead(ahead_sign, steps), theirs)

    def on_root(root):
        return root // NC == batch_pos // NC

    def after(array, earlier):
        return lax.optimization_barrier((array, earlier))[0]

    def both(*arrays):
        return lax.optimization_barrier(arrays)

    *early, lam_got = both(*[swapped[k] for k in range(far, 0, -1)], lam_got)
    swapped.update(zip(range(far, 0, -1), early))
    lam_pair = jnp.stack([own, lam_got])
    lam = jnp.stack([lam_pair, send(lam_pair, SWAP_YL)], axis=1).reshape(2 * NYL * local_b, width)
    give_own = inject(root_own, far, swapped[far])

    occ_energy, virt_energy, _ = both(occ_energy, virt_energy, give_own)
    pairs = jnp.concatenate(
        [lax.dynamic_index_in_dim(p, core, 0) for p in (pair_list, pair_list_other)]
    )
    occ_sum = occ_energy[pairs[:, 0]] + occ_energy[pairs[:, 1]] + occ_energy[owned_occ[root_own]]
    energy_b = lax.dynamic_slice_in_dim(virt_energy, slab_pos * local_b, local_b)
    energy_c = virt_energy[:window]
    base = ((occ_sum[:, None, None] - energy_c) - energy_b[:, None]).reshape(2, n_rows)
    last = (NZ - 1) * piece
    spare = NZ * piece - n_rows
    base = jnp.concatenate(
        [base[:, :last], jnp.full((2, spare), 1e30, jnp.float32), base[:, last:]], axis=1
    ).reshape(2, NZ, piece)
    base = lax.dynamic_slice_in_dim(jnp.concatenate([base, base], axis=1), z, NZ, axis=1)
    base = jnp.where(up, jnp.roll(base[:, ::-1], 1, axis=1), base)
    ea = virt_energy.reshape(NX, NYL, local_b)
    ea = jnp.where(yl == 0, ea, ea[:, ::-1])
    ea = lax.dynamic_slice_in_dim(jnp.concatenate([ea, ea], axis=0), x, NX, axis=0)
    ea = jnp.stack([ea, ea], axis=1).reshape(NX * 2 * NYL * local_b, 1)

    got_own = send(give_own, Z_RING)
    give_other = got_other = None
    for k in range(far - 1, 0, -1):
        if give_other is not None:
            got_own = after(got_own, give_other)
        if k == far - 1:
            got_own, lam = both(got_own, lam)
            got_own, base, ea = both(got_own, base, ea)
        elif k == far - 3:
            got_own, lam_x[1], lam_x[NX - 1] = both(got_own, lam_x[1], lam_x[NX - 1])
            got_other, lam_x[2] = both(got_other, lam_x[2])
        give_own = jnp.where(on_root(root_own), inject(root_own, k, swapped[k]), got_own)
        got_own = send(give_own, Z_RING)
        if got_other is None:
            lam_x = {step: send(after(lam, give_own), x_by(-step)) for step in (1, NX - 1, 2)}
            give_other = inject(root_other, k, after(swapped[k], give_own))
        else:
            got_other = after(got_other, give_own)
            give_other = jnp.where(
                on_root(root_other), inject(root_other, k, swapped[k]), got_other
            )
        got_other = send(give_other, Z_RING)
    crossed = send(after(got_other, got_own), SWAP_CORE)
    along = ((z - root_own // (NC * NYH)) * ahead_sign) % NZ
    mine = jnp.where(
        on_root(root_own),
        inject(root_own, 0, swapped[0]),
        jnp.where(along <= far, got_own, crossed),
    )
    here = jnp.where((root_own // NC) % NYH == yh, mine, send(mine, SWAP_YH))
    lams = [lam, lam_x[1], lam_x[2], lam_x[NX - 1]]

    def base_of(order):
        return jnp.concatenate([base[:, k] for k in order], axis=1)

    here, *lams = both(here, *lams)
    ring_own, ring_other, crossed = [here], [send(here, SWAP_CORE)], [here]

    total, lam = triples_call(base_of([0]), ea, lams, None, [here])
    for k in range(1, far):
        if k == 2:
            ring_own[-1], total = both(ring_own[-1], total)
        ring_own.append(send(ring_own[-1], Z_RING))
        if k == 3:
            first = [after(ring_own[1], ring_own[2]), crossed[1]]
            (total,) = triples_call(base_of([1, 7]), ea, lam, total, first)
            ring_other[-1], total = both(ring_other[-1], total)
        ring_other.append(send(after(ring_other[-1], ring_own[k - 1]), Z_RING))
        if k < far - 1:
            crossed.append(send(ring_other[-1], SWAP_CORE))
    farthest = send(ring_own[-1], Z_RING)
    middle = [after(ring_own[2], ring_own[3]), crossed[2]]
    (total,) = triples_call(base_of([2, 6]), ea, lam, total, middle)
    late = [ring_own[3], send(after(ring_other[3], total), SWAP_CORE), farthest]
    kept, *by_x, kept_y, by_y = triples_call(base_of([3, 5, 4]), ea, lam, total, late, last=True)

    got_y = send(by_y, SWAP_YL)
    got_x = [send(by_x[step - 1], x_by(step)) for step in (2, 1, 3)]
    other, *coded = recode(kept_y, got_y)
    own = kept + sum(decode(got, width) for got in got_x)
    own = own[:local_b] + send(own[local_b:], SWAP_YL)
    got_x = [send(coded[step - 1], x_by(step)) for step in (2, 1, 3)]
    other = send(other + sum(decode(got, width) for got in got_x), SWAP_CORE)
    return jnp.where(up, jnp.stack([own, other]), jnp.stack([other, own]))


def solution(mesh):
    placed = (
        P("batch", "slab", None),
        P("batch", "slab", None),
        P("batch", None),
        P(),
        P(),
        P(),
        P(),
    )
    return jax.shard_map(
        body, mesh=mesh, in_specs=placed, out_specs=P("batch", "slab", None), check_vma=False
    )
```

```python
import functools

import jax
import jax.numpy as jnp
from jax import lax
from jax.experimental import pallas as pl
from jax.experimental.pallas import tpu as pltpu
from jax.sharding import PartitionSpec as P

AXES = ("batch", "slab")
NZ, NYH, NC, NX, NYL = 8, 2, 2, 4, 2


def full_perm(move):
    pairs = []
    for device in range(NZ * NYH * NC * NX * NYL):
        rest, yl = divmod(device, NYL)
        rest, x = divmod(rest, NX)
        rest, core = divmod(rest, NC)
        z, yh = divmod(rest, NYH)
        z, yh, core, x, yl = move(z, yh, core, x, yl)
        target = (((z % NZ) * NYH + yh % NYH) * NC + core % NC) * NX + x % NX
        pairs.append((device, target * NYL + yl % NYL))
    return pairs


SWAP_CORE = full_perm(lambda z, h, c, x, l: (z, h, 1 - c, x, l))
SWAP_YH = full_perm(lambda z, h, c, x, l: (z, 1 - h, c, x, l))
SWAP_YL = full_perm(lambda z, h, c, x, l: (z, h, c, x, 1 - l))
Z_RING = full_perm(lambda z, h, c, x, l: (z + 1 - 2 * c, h, c, x, l))


def x_by(step):
    return full_perm(lambda z, h, c, x, l: (z, h, c, x + step, l))


def send(array, perm):
    return lax.ppermute(array, AXES, perm)


def encode(value, wide):
    top = jnp.maximum(jnp.max(jnp.abs(value), axis=1, keepdims=True), 2.0**-110)
    exponent = jnp.ceil(jnp.log(top * 1.0001) * 1.4426950408889634) - 15.0
    coded = jnp.floor(value * jnp.exp2(-exponent) + 0.5)
    tail = jnp.broadcast_to(exponent, (value.shape[0], wide - value.shape[1]))
    return jnp.concatenate([coded, tail], axis=1).astype(jnp.int32).astype(jnp.int16)


def decode(coded, width):
    coded = coded.astype(jnp.float32)
    return coded[:, :width] * jnp.exp2(coded[:, width : width + 1])


def triples_kernel(n_pieces, first, last, chunk, *refs):
    base_ref, ea_ref = refs[:2]
    if first:
        lam_refs = refs[2 : 2 + NX]
        at = 2 + NX
    else:
        lam_ref, prev_ref = refs[2:4]
        at = 4
    pieces = refs[at : at + n_pieces]
    outs = refs[at + n_pieces : len(refs) - 1]
    block_ref = refs[-1]
    g = pl.program_id(0)

    @pl.when(g == 0)
    def _():
        to = 0
        for piece in pieces:
            rows = piece.shape[0]
            block_ref[to : to + rows, :] = piece[...]
            to += rows

    if last:
        kept_ref, *by_x_refs, kept_y_ref, by_y_ref, total_ref = outs
    elif not first:
        (total_ref,) = outs
    else:
        total_ref, lam_ref = outs
        for k in range(NX):

            @pl.when(g == k)
            def _():
                lam_ref[...] = lam_refs[k][...]

    lam = lam_ref[...]
    part = lam.shape[0] // 2
    rows = block_ref.shape[0]
    for at in range(0, rows, chunk):
        size = min(chunk, rows - at)
        block = block_ref[at : at + size, :]
        weighted = lax.dot_general(
            lam, block, (((1,), (1,)), ((), ())), preferred_element_type=jnp.float32
        )
        divided = []
        for k in range(2):
            denom = base_ref[k : k + 1, at : at + size] - ea_ref[k * part : (k + 1) * part, :]
            inverse = pl.reciprocal(denom, approx=True)
            inverse = inverse * (2.0 - denom * inverse)
            divided.append(weighted[k * part : (k + 1) * part] * inverse)
        triples = jnp.concatenate(divided, axis=0).astype(jnp.bfloat16)
        share = jnp.dot(triples, block, preferred_element_type=jnp.float32)
        if at:
            total_ref[...] += share
        elif first:
            total_ref[...] = share
        else:
            total_ref[...] = prev_ref[...] + share
    if not last:
        return
    wide = by_y_ref.shape[2]
    mid = part + part // 2

    @pl.when(g == 0)
    def _():
        kept_ref[...] = total_ref[:part, :]

    for k in range(1, NX):

        @pl.when(g == k)
        def _():
            by_x_refs[k - 1][...] = encode(total_ref[:part, :], wide)

    kept_y_ref[0] = total_ref[part:mid, :]
    by_y_ref[0] = encode(total_ref[mid:, :], wide)


def whole(shape):
    return pl.BlockSpec(shape, lambda g: (0,) * len(shape))


def held(shape):
    return pl.BlockSpec(shape, lambda g: (0,) * len(shape), pipeline_mode=pl.Buffered(1))


def by_step(shape):
    return pl.BlockSpec((1,) + shape[1:], lambda g: (g, 0, 0))


def triples_call(base, ea, lams, prev, pieces, last=False):
    first = prev is None
    rows = sum(p.shape[0] for p in pieces)
    tile, width = lams[0].shape if first else (lams.shape[0] // NX, lams.shape[1])
    padded = -(-rows // 128) * 128
    base = jnp.pad(base, ((0, 0), (0, padded - rows)), constant_values=1.0)
    spec = pl.BlockSpec((tile, width), lambda g: (g, 0))
    in_specs = [held(base.shape), pl.BlockSpec((tile, 1), lambda g: (g, 0))]
    in_specs += [held(p.shape) for p in lams] if first else [spec, spec]
    in_specs += [held(p.shape) for p in pieces]
    args = [base, ea, *(lams if first else [lams, prev]), *pieces]
    scratch = [pltpu.VMEM((rows, width), jnp.bfloat16)]
    if last:
        half = tile // 2
        wide = -(-(width + 1) // 128) * 128
        shapes = [((half, width), jnp.float32)] + [((half, wide), jnp.int16)] * (NX - 1)
        out_specs = [whole(shape) for shape, _ in shapes]
        pair = [((NX, half // 2, width), jnp.float32), ((NX, half // 2, wide), jnp.int16)]
        out_specs += [by_step(shape) for shape, _ in pair]
        shapes += pair
        scratch = [pltpu.VMEM((tile, width), jnp.float32)] + scratch
    else:
        shapes = [((NX * tile, width), jnp.float32), ((NX * tile, width), jnp.bfloat16)]
        shapes = shapes[: 1 + first]
        out_specs = [spec] * len(shapes)
    return pl.pallas_call(
        functools.partial(triples_kernel, len(pieces), first, last, 512),
        grid=(NX,),
        in_specs=in_specs,
        out_specs=out_specs,
        out_shape=[jax.ShapeDtypeStruct(*shape) for shape in shapes],
        scratch_shapes=scratch,
        compiler_params=pltpu.CompilerParams(vmem_limit_bytes=24 * 1024 * 1024),
        cost_estimate=pl.CostEstimate(
            flops=4 * rows * NX * tile * width,
            bytes_accessed=2 * rows * width + 10 * NX * tile * width,
            transcendentals=0,
        ),
    )(*args)


def recode_kernel(kept_ref, got_ref, own_ref, *coded_refs):
    g = pl.program_id(0)
    total = kept_ref[0] + decode(got_ref[0], kept_ref.shape[2])

    @pl.when(g == 0)
    def _():
        own_ref[...] = total

    for k in range(1, NX):

        @pl.when(g == k)
        def _():
            coded_refs[k - 1][...] = encode(total, got_ref.shape[2])


def recode(kept, got):
    shapes = [(kept.shape[1:], jnp.float32)] + [(got.shape[1:], jnp.int16)] * (NX - 1)
    return pl.pallas_call(
        recode_kernel,
        grid=(NX,),
        in_specs=[by_step(kept.shape), by_step(got.shape)],
        out_specs=[whole(shape) for shape, _ in shapes],
        out_shape=[jax.ShapeDtypeStruct(*shape) for shape in shapes],
        compiler_params=pltpu.CompilerParams(vmem_limit_bytes=16 * 1024 * 1024),
        cost_estimate=pl.CostEstimate(
            flops=10 * kept.size, bytes_accessed=10 * kept.size, transcendentals=0
        ),
    )(kept, got)


def body(lambda_pairs, vvvo, pair_list, owned_occ, step_root, occ_energy, virt_energy):
    window, local_b, width = vvvo.shape
    n_rows = window * local_b
    batch_pos = lax.axis_index("batch")
    slab_pos = lax.axis_index("slab")
    core = batch_pos % NC
    yh = (batch_pos // NC) % NYH
    z = batch_pos // (NC * NYH)
    x = slab_pos // NYL
    yl = slab_pos % NYL
    up = core == 0
    ahead_sign = 1 - 2 * core
    root_own = jnp.where(up, step_root[0], step_root[1])
    root_other = jnp.where(up, step_root[1], step_root[0])

    pair_list_other = send(pair_list, SWAP_CORE)

    lam = jnp.stack([lambda_pairs, send(lambda_pairs, SWAP_YL)], axis=1)
    lam = lam.reshape(2 * NYL * local_b, width)

    flat = vvvo.transpose(1, 0, 2).reshape(n_rows, width)
    far = NZ // 2

    piece = -(-n_rows // (NZ * 16)) * 16

    def ahead(sign, steps):
        start = jnp.minimum((z + sign * steps) % NZ * piece, n_rows - piece)
        return lax.dynamic_slice_in_dim(flat, start, piece)

    swapped = {k: send(ahead(-ahead_sign, k), SWAP_CORE) for k in range(far, -1, -1)}

    def inject(root, steps, theirs):
        return jnp.where(root % NC == core, ahead(ahead_sign, steps), theirs)

    def on_root(root):
        return root // NC == batch_pos // NC

    def after(array, earlier):
        return lax.optimization_barrier((array, earlier))[0]

    def both(*arrays):
        return lax.optimization_barrier(arrays)

    early = both(*[swapped[k] for k in range(far, 0, -1)])
    swapped.update(zip(range(far, 0, -1), early))
    give_own = inject(root_own, far, swapped[far])

    def energies(earlier):
        occ, virt, pairs, pairs_other, holds, _ = both(
            occ_energy, virt_energy, pair_list, pair_list_other, owned_occ, earlier
        )
        pairs = jnp.concatenate(
            [lax.dynamic_index_in_dim(p, core, 0) for p in (pairs, pairs_other)]
        )
        occ_sum = occ[pairs[:, 0]] + occ[pairs[:, 1]] + occ[holds[root_own]]
        energy_b = lax.dynamic_slice_in_dim(virt, slab_pos * local_b, local_b)
        energy_c = virt[:window]
        base = ((occ_sum[:, None, None] - energy_c) - energy_b[:, None]).reshape(2, n_rows)
        last = (NZ - 1) * piece
        spare = NZ * piece - n_rows
        base = jnp.concatenate(
            [base[:, :last], jnp.full((2, spare), 1e30, jnp.float32), base[:, last:]], axis=1
        ).reshape(2, NZ, piece)
        base = lax.dynamic_slice_in_dim(jnp.concatenate([base, base], axis=1), z, NZ, axis=1)
        base = jnp.where(up, jnp.roll(base[:, ::-1], 1, axis=1), base)
        ea = virt.reshape(NX, NYL, local_b)
        ea = jnp.where(yl == 0, ea, ea[:, ::-1])
        ea = lax.dynamic_slice_in_dim(jnp.concatenate([ea, ea], axis=0), x, NX, axis=0)
        ea = jnp.stack([ea, ea], axis=1).reshape(NX * 2 * NYL * local_b, 1)
        return base, ea

    got_own = send(give_own, Z_RING)
    give_other = got_other = None
    for k in range(far - 1, 0, -1):
        if give_other is not None:
            got_own = after(got_own, give_other)
        if k == far - 1:
            got_own, lam = both(got_own, lam)
            lam_x = {step: send(lam, x_by(-step)) for step in (1, NX - 1, 2)}
        elif k == far - 2:
            got_own, lam_x[1], lam_x[NX - 1] = both(got_own, lam_x[1], lam_x[NX - 1])
        elif k == far - 3:
            got_own, lam_x[2] = both(got_own, lam_x[2])
        give_own = jnp.where(on_root(root_own), inject(root_own, k, swapped[k]), got_own)
        got_own = send(give_own, Z_RING)
        if got_other is None:
            give_other = inject(root_other, k, after(swapped[k], give_own))
        else:
            got_other = after(got_other, give_own)
            give_other = jnp.where(
                on_root(root_other), inject(root_other, k, swapped[k]), got_other
            )
        got_other = send(give_other, Z_RING)
    crossed = send(after(got_other, got_own), SWAP_CORE)
    along = ((z - root_own // (NC * NYH)) * ahead_sign) % NZ
    mine = jnp.where(
        on_root(root_own),
        inject(root_own, 0, swapped[0]),
        jnp.where(along <= far, got_own, crossed),
    )
    here = jnp.where((root_own // NC) % NYH == yh, mine, send(mine, SWAP_YH))

    lams = []
    for rows in (lam, lam_x[1], lam_x[2], lam_x[NX - 1]):
        rows = after(rows, mine).reshape(2, NYL * local_b, width)
        give = lax.dynamic_index_in_dim(rows, 1 - core, 0, keepdims=False)
        own = lax.dynamic_index_in_dim(rows, core, 0, keepdims=False)
        lams.append(jnp.concatenate([own, send(give, SWAP_CORE)]))

    here, *lams = both(here, *lams)
    ring_own, ring_other, crossed = [here], [send(here, SWAP_CORE)], [here]

    base, ea = energies(ring_other[0])

    def base_of(order):
        return jnp.concatenate([base[:, k] for k in order], axis=1)

    for k in range(1, far):
        ring_own.append(send(ring_own[-1], Z_RING))
        if k == 3:
            first = [here, after(ring_own[1], ring_own[2]), crossed[1]]
            total, lam = triples_call(base_of([0, 1, 7]), ea, lams, None, first)
            ring_other[-1], total = both(ring_other[-1], total)
            crossed.append(send(ring_other[-1], SWAP_CORE))
        ring_other.append(send(after(ring_other[-1], ring_own[k - 1]), Z_RING))
        if k == 1:
            crossed.append(send(ring_other[-1], SWAP_CORE))
    farthest = send(ring_own[-1], Z_RING)
    middle = [after(ring_own[2], ring_own[3]), crossed[2]]
    (total,) = triples_call(base_of([2, 6]), ea, lam, total, middle)
    late = [ring_own[3], send(after(ring_other[3], total), SWAP_CORE), farthest]
    kept, *by_x, kept_y, by_y = triples_call(base_of([3, 5, 4]), ea, lam, total, late, last=True)

    got_y = send(by_y, SWAP_YL)
    got_x = [send(by_x[step - 1], x_by(step)) for step in (2, 1, 3)]
    other, *coded = recode(kept_y, got_y)
    own = kept + sum(decode(got, width) for got in got_x)
    own = own[:local_b] + send(own[local_b:], SWAP_YL)
    got_x = [send(coded[step - 1], x_by(step)) for step in (2, 1, 3)]
    other = send(other + sum(decode(got, width) for got in got_x), SWAP_CORE)
    return jnp.where(up, jnp.stack([own, other]), jnp.stack([other, own]))


def solution(mesh):
    placed = (
        P("batch", "slab", None),
        P("batch", "slab", None),
        P("batch", None),
        P(),
        P(),
        P(),
        P(),
    )
    return jax.shard_map(
        body, mesh=mesh, in_specs=placed, out_specs=P("batch", "slab", None), check_vma=False
    )
```

```python
import functools

import jax
import jax.numpy as jnp
from jax import lax
from jax.experimental import pallas as pl
from jax.experimental.pallas import tpu as pltpu
from jax.sharding import PartitionSpec as P

AXES = ("batch", "slab")
NZ, NYH, NC, NX, NYL = 8, 2, 2, 4, 2


def full_perm(move):
    pairs = []
    for device in range(NZ * NYH * NC * NX * NYL):
        rest, yl = divmod(device, NYL)
        rest, x = divmod(rest, NX)
        rest, core = divmod(rest, NC)
        z, yh = divmod(rest, NYH)
        z, yh, core, x, yl = move(z, yh, core, x, yl)
        target = (((z % NZ) * NYH + yh % NYH) * NC + core % NC) * NX + x % NX
        pairs.append((device, target * NYL + yl % NYL))
    return pairs


SWAP_CORE = full_perm(lambda z, h, c, x, l: (z, h, 1 - c, x, l))
SWAP_YH = full_perm(lambda z, h, c, x, l: (z, 1 - h, c, x, l))
SWAP_YL = full_perm(lambda z, h, c, x, l: (z, h, c, x, 1 - l))
Z_RING = full_perm(lambda z, h, c, x, l: (z + 1 - 2 * c, h, c, x, l))


def x_by(step):
    return full_perm(lambda z, h, c, x, l: (z, h, c, x + step, l))


def send(array, perm):
    return lax.ppermute(array, AXES, perm)


def encode(value, wide):
    top = jnp.maximum(jnp.max(jnp.abs(value), axis=1, keepdims=True), 2.0**-110)
    exponent = jnp.ceil(jnp.log(top * 1.0001) * 1.4426950408889634) - 15.0
    coded = jnp.floor(value * jnp.exp2(-exponent) + 0.5)
    tail = jnp.broadcast_to(exponent, (value.shape[0], wide - value.shape[1]))
    return jnp.concatenate([coded, tail], axis=1).astype(jnp.int32).astype(jnp.int16)


def decode(coded, width):
    coded = coded.astype(jnp.float32)
    return coded[:, :width] * jnp.exp2(coded[:, width : width + 1])


def triples_kernel(n_pieces, first, last, chunk, *refs):
    base_ref, ea_ref = refs[:2]
    if first:
        lam_refs = refs[2 : 2 + NX]
        at = 2 + NX
    else:
        lam_ref, prev_ref = refs[2:4]
        at = 4
    pieces = refs[at : at + n_pieces]
    outs = refs[at + n_pieces : len(refs) - 1]
    block_ref = refs[-1]
    g = pl.program_id(0)

    @pl.when(g == 0)
    def _():
        to = 0
        for piece in pieces:
            rows = piece.shape[0]
            block_ref[to : to + rows, :] = piece[...]
            to += rows

    if last:
        kept_ref, *by_x_refs, kept_y_ref, by_y_ref, total_ref = outs
    elif not first:
        (total_ref,) = outs
    else:
        total_ref, lam_ref = outs
        for k in range(NX):

            @pl.when(g == k)
            def _():
                lam_ref[...] = lam_refs[k][...]

    lam = lam_ref[...]
    part = lam.shape[0] // 2
    rows = block_ref.shape[0]
    for at in range(0, rows, chunk):
        size = min(chunk, rows - at)
        block = block_ref[at : at + size, :]
        weighted = lax.dot_general(
            lam, block, (((1,), (1,)), ((), ())), preferred_element_type=jnp.float32
        )
        divided = []
        for k in range(2):
            denom = base_ref[k : k + 1, at : at + size] - ea_ref[k * part : (k + 1) * part, :]
            inverse = pl.reciprocal(denom, approx=True)
            inverse = inverse * (2.0 - denom * inverse)
            divided.append(weighted[k * part : (k + 1) * part] * inverse)
        triples = jnp.concatenate(divided, axis=0).astype(jnp.bfloat16)
        share = jnp.dot(triples, block, preferred_element_type=jnp.float32)
        if at:
            total_ref[...] += share
        elif first:
            total_ref[...] = share
        else:
            total_ref[...] = prev_ref[...] + share
    if not last:
        return
    wide = by_y_ref.shape[2]
    mid = part + part // 2

    @pl.when(g == 0)
    def _():
        kept_ref[...] = total_ref[:part, :]

    for k in range(1, NX):

        @pl.when(g == k)
        def _():
            by_x_refs[k - 1][...] = encode(total_ref[:part, :], wide)

    kept_y_ref[0] = total_ref[part:mid, :]
    by_y_ref[0] = encode(total_ref[mid:, :], wide)


def whole(shape):
    return pl.BlockSpec(shape, lambda g: (0,) * len(shape))


def held(shape):
    return pl.BlockSpec(shape, lambda g: (0,) * len(shape), pipeline_mode=pl.Buffered(1))


def by_step(shape):
    return pl.BlockSpec((1,) + shape[1:], lambda g: (g, 0, 0))


def triples_call(base, ea, lams, prev, pieces, last=False):
    first = prev is None
    rows = sum(p.shape[0] for p in pieces)
    tile, width = lams[0].shape if first else (lams.shape[0] // NX, lams.shape[1])
    padded = -(-rows // 128) * 128
    base = jnp.pad(base, ((0, 0), (0, padded - rows)), constant_values=1.0)
    spec = pl.BlockSpec((tile, width), lambda g: (g, 0))
    in_specs = [held(base.shape), pl.BlockSpec((tile, 1), lambda g: (g, 0))]
    in_specs += [held(p.shape) for p in lams] if first else [spec, spec]
    in_specs += [held(p.shape) for p in pieces]
    args = [base, ea, *(lams if first else [lams, prev]), *pieces]
    scratch = [pltpu.VMEM((rows, width), jnp.bfloat16)]
    if last:
        half = tile // 2
        wide = -(-(width + 1) // 128) * 128
        shapes = [((half, width), jnp.float32)] + [((half, wide), jnp.int16)] * (NX - 1)
        out_specs = [whole(shape) for shape, _ in shapes]
        pair = [((NX, half // 2, width), jnp.float32), ((NX, half // 2, wide), jnp.int16)]
        out_specs += [by_step(shape) for shape, _ in pair]
        shapes += pair
        scratch = [pltpu.VMEM((tile, width), jnp.float32)] + scratch
    else:
        shapes = [((NX * tile, width), jnp.float32), ((NX * tile, width), jnp.bfloat16)]
        shapes = shapes[: 1 + first]
        out_specs = [spec] * len(shapes)
    return pl.pallas_call(
        functools.partial(triples_kernel, len(pieces), first, last, 512),
        grid=(NX,),
        in_specs=in_specs,
        out_specs=out_specs,
        out_shape=[jax.ShapeDtypeStruct(*shape) for shape in shapes],
        scratch_shapes=scratch,
        compiler_params=pltpu.CompilerParams(vmem_limit_bytes=24 * 1024 * 1024),
        cost_estimate=pl.CostEstimate(
            flops=4 * rows * NX * tile * width,
            bytes_accessed=2 * rows * width + 10 * NX * tile * width,
            transcendentals=0,
        ),
    )(*args)


def recode_kernel(kept_ref, got_ref, own_ref, *coded_refs):
    g = pl.program_id(0)
    total = kept_ref[0] + decode(got_ref[0], kept_ref.shape[2])

    @pl.when(g == 0)
    def _():
        own_ref[...] = total

    for k in range(1, NX):

        @pl.when(g == k)
        def _():
            coded_refs[k - 1][...] = encode(total, got_ref.shape[2])


def recode(kept, got):
    shapes = [(kept.shape[1:], jnp.float32)] + [(got.shape[1:], jnp.int16)] * (NX - 1)
    return pl.pallas_call(
        recode_kernel,
        grid=(NX,),
        in_specs=[by_step(kept.shape), by_step(got.shape)],
        out_specs=[whole(shape) for shape, _ in shapes],
        out_shape=[jax.ShapeDtypeStruct(*shape) for shape in shapes],
        compiler_params=pltpu.CompilerParams(vmem_limit_bytes=16 * 1024 * 1024),
        cost_estimate=pl.CostEstimate(
            flops=10 * kept.size, bytes_accessed=10 * kept.size, transcendentals=0
        ),
    )(kept, got)


def body(lambda_pairs, vvvo, pair_list, owned_occ, step_root, occ_energy, virt_energy):
    window, local_b, width = vvvo.shape
    n_rows = window * local_b
    batch_pos = lax.axis_index("batch")
    slab_pos = lax.axis_index("slab")
    core = batch_pos % NC
    yh = (batch_pos // NC) % NYH
    z = batch_pos // (NC * NYH)
    x = slab_pos // NYL
    yl = slab_pos % NYL
    up = core == 0
    ahead_sign = 1 - 2 * core
    root_own = jnp.where(up, step_root[0], step_root[1])
    root_other = jnp.where(up, step_root[1], step_root[0])

    pair_list_other = send(pair_list, SWAP_CORE)

    lam = jnp.stack([lambda_pairs, send(lambda_pairs, SWAP_YL)], axis=1)
    lam = lam.reshape(2 * NYL * local_b, width)

    flat = vvvo.transpose(1, 0, 2).reshape(n_rows, width)
    far = NZ // 2

    piece = -(-n_rows // (NZ * 16)) * 16

    def ahead(sign, steps):
        start = jnp.minimum((z + sign * steps) % NZ * piece, n_rows - piece)
        return lax.dynamic_slice_in_dim(flat, start, piece)

    swapped = {k: send(ahead(-ahead_sign, k), SWAP_CORE) for k in range(far, -1, -1)}

    def inject(root, steps, theirs):
        return jnp.where(root % NC == core, ahead(ahead_sign, steps), theirs)

    def on_root(root):
        return root // NC == batch_pos // NC

    def after(array, earlier):
        return lax.optimization_barrier((array, earlier))[0]

    def both(*arrays):
        return lax.optimization_barrier(arrays)

    early = both(*[swapped[k] for k in range(far, 0, -1)])
    swapped.update(zip(range(far, 0, -1), early))
    give_own = inject(root_own, far, swapped[far])

    def energies(earlier):
        occ, virt, pairs, pairs_other, holds, _ = both(
            occ_energy, virt_energy, pair_list, pair_list_other, owned_occ, earlier
        )
        pairs = jnp.concatenate(
            [lax.dynamic_index_in_dim(p, core, 0) for p in (pairs, pairs_other)]
        )
        occ_sum = occ[pairs[:, 0]] + occ[pairs[:, 1]] + occ[holds[root_own]]
        energy_b = lax.dynamic_slice_in_dim(virt, slab_pos * local_b, local_b)
        energy_c = virt[:window]
        base = ((occ_sum[:, None, None] - energy_c) - energy_b[:, None]).reshape(2, n_rows)
        last = (NZ - 1) * piece
        spare = NZ * piece - n_rows
        base = jnp.concatenate(
            [base[:, :last], jnp.full((2, spare), 1e30, jnp.float32), base[:, last:]], axis=1
        ).reshape(2, NZ, piece)
        base = lax.dynamic_slice_in_dim(jnp.concatenate([base, base], axis=1), z, NZ, axis=1)
        base = jnp.where(up, jnp.roll(base[:, ::-1], 1, axis=1), base)
        ea = virt.reshape(NX, NYL, local_b)
        ea = jnp.where(yl == 0, ea, ea[:, ::-1])
        ea = lax.dynamic_slice_in_dim(jnp.concatenate([ea, ea], axis=0), x, NX, axis=0)
        ea = jnp.stack([ea, ea], axis=1).reshape(NX * 2 * NYL * local_b, 1)
        return base, ea

    got_own = send(give_own, Z_RING)
    give_other = got_other = None
    for k in range(far - 1, 0, -1):
        if give_other is not None:
            got_own = after(got_own, give_other)
        if k == far - 1:
            got_own, lam = both(got_own, lam)
            lam_up, lam_down = send(lam, x_by(-1)), send(lam, x_by(1))
        elif k == far - 2:
            got_other, lam_up, lam_down = both(got_other, lam_up, lam_down)
            lam_far = [send(lam_up[: NYL * local_b], x_by(-1))]
            lam_far.append(send(lam_down[NYL * local_b :], x_by(1)))
        elif k == far - 3:
            got_other, *lam_far = both(got_other, *lam_far)
        give_own = jnp.where(on_root(root_own), inject(root_own, k, swapped[k]), got_own)
        got_own = send(give_own, Z_RING)
        if got_other is None:
            give_other = inject(root_other, k, after(swapped[k], give_own))
        else:
            got_other = after(got_other, give_own)
            give_other = jnp.where(
                on_root(root_other), inject(root_other, k, swapped[k]), got_other
            )
        got_other = send(give_other, Z_RING)
    crossed = send(after(got_other, got_own), SWAP_CORE)
    along = ((z - root_own // (NC * NYH)) * ahead_sign) % NZ
    mine = jnp.where(
        on_root(root_own),
        inject(root_own, 0, swapped[0]),
        jnp.where(along <= far, got_own, crossed),
    )
    here = jnp.where((root_own // NC) % NYH == yh, mine, send(mine, SWAP_YH))

    lams = []
    for rows in (lam, lam_up, lam_far, lam_down):
        if rows is not lam_far:
            rows = [rows[: NYL * local_b], rows[NYL * local_b :]]
        first, second = both(*rows, mine)[:2]
        got = send(jnp.where(up, second, first), SWAP_CORE)
        lams.append(jnp.concatenate([jnp.where(up, first, second), got]))
    base, ea = energies(got)

    here, base, ea, *lams = both(here, base, ea, *lams)
    ring_own, ring_other, crossed = [here], [send(here, SWAP_CORE)], [here]

    def base_of(order):
        return jnp.concatenate([base[:, k] for k in order], axis=1)

    total, lam = triples_call(base_of([0]), ea, lams, None, [here])
    for k in range(1, far):
        if k == 2:
            ring_own[-1], total = both(ring_own[-1], total)
        ring_own.append(send(ring_own[-1], Z_RING))
        if k == 3:
            first = [after(ring_own[1], ring_own[2]), crossed[1]]
            (total,) = triples_call(base_of([1, 7]), ea, lam, total, first)
            ring_other[-1], total = both(ring_other[-1], total)
            crossed.append(send(ring_other[-1], SWAP_CORE))
        ring_other.append(send(after(ring_other[-1], ring_own[k - 1]), Z_RING))
        if k == 1:
            crossed.append(send(ring_other[-1], SWAP_CORE))
    farthest = send(ring_own[-1], Z_RING)
    middle = [after(ring_own[2], ring_own[3]), crossed[2]]
    (total,) = triples_call(base_of([2, 6]), ea, lam, total, middle)
    late = [ring_own[3], send(after(ring_other[3], total), SWAP_CORE), farthest]
    kept, *by_x, kept_y, by_y = triples_call(base_of([3, 5, 4]), ea, lam, total, late, last=True)

    got_y = send(by_y, SWAP_YL)
    got_x = [send(by_x[step - 1], x_by(step)) for step in (2, 1, 3)]
    other, *coded = recode(kept_y, got_y)
    own = kept + sum(decode(got, width) for got in got_x)
    own = own[:local_b] + send(own[local_b:], SWAP_YL)
    got_x = [send(coded[step - 1], x_by(step)) for step in (2, 1, 3)]
    other = send(other + sum(decode(got, width) for got in got_x), SWAP_CORE)
    return jnp.where(up, jnp.stack([own, other]), jnp.stack([other, own]))


def solution(mesh):
    placed = (
        P("batch", "slab", None),
        P("batch", "slab", None),
        P("batch", None),
        P(),
        P(),
        P(),
        P(),
    )
    return jax.shard_map(
        body, mesh=mesh, in_specs=placed, out_specs=P("batch", "slab", None), check_vma=False
    )
```

```python
import functools

import jax
import jax.numpy as jnp
from jax import lax
from jax.experimental import pallas as pl
from jax.experimental.pallas import tpu as pltpu
from jax.sharding import PartitionSpec as P

AXES = ("batch", "slab")
NZ, NYH, NC, NX, NYL = 8, 2, 2, 4, 2


def full_perm(move):
    pairs = []
    for device in range(NZ * NYH * NC * NX * NYL):
        rest, yl = divmod(device, NYL)
        rest, x = divmod(rest, NX)
        rest, core = divmod(rest, NC)
        z, yh = divmod(rest, NYH)
        z, yh, core, x, yl = move(z, yh, core, x, yl)
        target = (((z % NZ) * NYH + yh % NYH) * NC + core % NC) * NX + x % NX
        pairs.append((device, target * NYL + yl % NYL))
    return pairs


SWAP_CORE = full_perm(lambda z, h, c, x, l: (z, h, 1 - c, x, l))
SWAP_YH = full_perm(lambda z, h, c, x, l: (z, 1 - h, c, x, l))
SWAP_YL = full_perm(lambda z, h, c, x, l: (z, h, c, x, 1 - l))
Z_RING = full_perm(lambda z, h, c, x, l: (z + 1 - 2 * c, h, c, x, l))


def x_by(step):
    return full_perm(lambda z, h, c, x, l: (z, h, c, x + step, l))


def send(array, perm):
    return lax.ppermute(array, AXES, perm)


def encode(value, wide):
    top = jnp.maximum(jnp.max(jnp.abs(value), axis=1, keepdims=True), 2.0**-110)
    exponent = jnp.ceil(jnp.log(top * 1.0001) * 1.4426950408889634) - 15.0
    coded = jnp.floor(value * jnp.exp2(-exponent) + 0.5)
    tail = jnp.broadcast_to(exponent, (value.shape[0], wide - value.shape[1]))
    return jnp.concatenate([coded, tail], axis=1).astype(jnp.int32).astype(jnp.int16)


def decode(coded, width):
    coded = coded.astype(jnp.float32)
    return coded[:, :width] * jnp.exp2(coded[:, width : width + 1])


def triples_kernel(n_pieces, first, last, chunk, *refs):
    base_ref, ea_ref = refs[:2]
    if first:
        lam_refs = refs[2 : 2 + NX]
        at = 2 + NX
    else:
        lam_ref, prev_ref = refs[2:4]
        at = 4
    pieces = refs[at : at + n_pieces]
    outs = refs[at + n_pieces : len(refs) - 1]
    block_ref = refs[-1]
    g = pl.program_id(0)

    @pl.when(g == 0)
    def _():
        to = 0
        for piece in pieces:
            rows = piece.shape[0]
            block_ref[to : to + rows, :] = piece[...]
            to += rows

    if last:
        kept_ref, *by_x_refs, kept_y_ref, by_y_ref, total_ref = outs
    elif not first:
        (total_ref,) = outs
    else:
        total_ref, lam_ref = outs
        for k in range(NX):

            @pl.when(g == k)
            def _():
                lam_ref[...] = lam_refs[k][...]

    lam = lam_ref[...]
    part = lam.shape[0] // 2
    rows = block_ref.shape[0]
    for at in range(0, rows, chunk):
        size = min(chunk, rows - at)
        block = block_ref[at : at + size, :]
        weighted = lax.dot_general(
            lam, block, (((1,), (1,)), ((), ())), preferred_element_type=jnp.float32
        )
        divided = []
        for k in range(2):
            denom = base_ref[k : k + 1, at : at + size] - ea_ref[k * part : (k + 1) * part, :]
            inverse = pl.reciprocal(denom, approx=True)
            inverse = inverse * (2.0 - denom * inverse)
            divided.append(weighted[k * part : (k + 1) * part] * inverse)
        triples = jnp.concatenate(divided, axis=0).astype(jnp.bfloat16)
        share = jnp.dot(triples, block, preferred_element_type=jnp.float32)
        if at:
            total_ref[...] += share
        elif first:
            total_ref[...] = share
        else:
            total_ref[...] = prev_ref[...] + share
    if not last:
        return
    wide = by_y_ref.shape[2]
    mid = part + part // 2

    @pl.when(g == 0)
    def _():
        kept_ref[...] = total_ref[:part, :]

    for k in range(1, NX):

        @pl.when(g == k)
        def _():
            by_x_refs[k - 1][...] = encode(total_ref[:part, :], wide)

    kept_y_ref[0] = total_ref[part:mid, :]
    by_y_ref[0] = encode(total_ref[mid:, :], wide)


def whole(shape):
    return pl.BlockSpec(shape, lambda g: (0,) * len(shape))


def held(shape):
    return pl.BlockSpec(shape, lambda g: (0,) * len(shape), pipeline_mode=pl.Buffered(1))


def by_step(shape):
    return pl.BlockSpec((1,) + shape[1:], lambda g: (g, 0, 0))


def triples_call(base, ea, lams, prev, pieces, last=False):
    first = prev is None
    rows = sum(p.shape[0] for p in pieces)
    tile, width = lams[0].shape if first else (lams.shape[0] // NX, lams.shape[1])
    padded = -(-rows // 128) * 128
    base = jnp.pad(base, ((0, 0), (0, padded - rows)), constant_values=1.0)
    spec = pl.BlockSpec((tile, width), lambda g: (g, 0))
    in_specs = [held(base.shape), pl.BlockSpec((tile, 1), lambda g: (g, 0))]
    in_specs += [held(p.shape) for p in lams] if first else [spec, spec]
    in_specs += [held(p.shape) for p in pieces]
    args = [base, ea, *(lams if first else [lams, prev]), *pieces]
    scratch = [pltpu.VMEM((rows, width), jnp.bfloat16)]
    if last:
        half = tile // 2
        wide = -(-(width + 1) // 128) * 128
        shapes = [((half, width), jnp.float32)] + [((half, wide), jnp.int16)] * (NX - 1)
        out_specs = [whole(shape) for shape, _ in shapes]
        pair = [((NX, half // 2, width), jnp.float32), ((NX, half // 2, wide), jnp.int16)]
        out_specs += [by_step(shape) for shape, _ in pair]
        shapes += pair
        scratch = [pltpu.VMEM((tile, width), jnp.float32)] + scratch
    else:
        shapes = [((NX * tile, width), jnp.float32), ((NX * tile, width), jnp.bfloat16)]
        shapes = shapes[: 1 + first]
        out_specs = [spec] * len(shapes)
    return pl.pallas_call(
        functools.partial(triples_kernel, len(pieces), first, last, 512),
        grid=(NX,),
        in_specs=in_specs,
        out_specs=out_specs,
        out_shape=[jax.ShapeDtypeStruct(*shape) for shape in shapes],
        scratch_shapes=scratch,
        compiler_params=pltpu.CompilerParams(vmem_limit_bytes=24 * 1024 * 1024),
        cost_estimate=pl.CostEstimate(
            flops=4 * rows * NX * tile * width,
            bytes_accessed=2 * rows * width + 10 * NX * tile * width,
            transcendentals=0,
        ),
    )(*args)


def recode_kernel(kept_ref, got_ref, own_ref, *coded_refs):
    g = pl.program_id(0)
    total = kept_ref[0] + decode(got_ref[0], kept_ref.shape[2])

    @pl.when(g == 0)
    def _():
        own_ref[...] = total

    for k in range(1, NX):

        @pl.when(g == k)
        def _():
            coded_refs[k - 1][...] = encode(total, got_ref.shape[2])


def recode(kept, got):
    shapes = [(kept.shape[1:], jnp.float32)] + [(got.shape[1:], jnp.int16)] * (NX - 1)
    return pl.pallas_call(
        recode_kernel,
        grid=(NX,),
        in_specs=[by_step(kept.shape), by_step(got.shape)],
        out_specs=[whole(shape) for shape, _ in shapes],
        out_shape=[jax.ShapeDtypeStruct(*shape) for shape in shapes],
        compiler_params=pltpu.CompilerParams(vmem_limit_bytes=16 * 1024 * 1024),
        cost_estimate=pl.CostEstimate(
            flops=10 * kept.size, bytes_accessed=10 * kept.size, transcendentals=0
        ),
    )(kept, got)


def body(lambda_pairs, vvvo, pair_list, owned_occ, step_root, occ_energy, virt_energy):
    window, local_b, width = vvvo.shape
    n_rows = window * local_b
    batch_pos = lax.axis_index("batch")
    slab_pos = lax.axis_index("slab")
    core = batch_pos % NC
    yh = (batch_pos // NC) % NYH
    z = batch_pos // (NC * NYH)
    x = slab_pos // NYL
    yl = slab_pos % NYL
    up = core == 0
    ahead_sign = 1 - 2 * core
    root_own = jnp.where(up, step_root[0], step_root[1])
    root_other = jnp.where(up, step_root[1], step_root[0])

    pair_list_other = send(pair_list, SWAP_CORE)

    lam = jnp.stack([lambda_pairs, send(lambda_pairs, SWAP_YL)], axis=1)
    lam = lam.reshape(2 * NYL * local_b, width)

    flat = vvvo.transpose(1, 0, 2).reshape(n_rows, width)
    far = NZ // 2

    piece = -(-n_rows // (NZ * 16)) * 16

    def ahead(sign, steps):
        start = jnp.minimum((z + sign * steps) % NZ * piece, n_rows - piece)
        return lax.dynamic_slice_in_dim(flat, start, piece)

    swapped = {k: send(ahead(-ahead_sign, k), SWAP_CORE) for k in range(far, -1, -1)}

    def inject(root, steps, theirs):
        return jnp.where(root % NC == core, ahead(ahead_sign, steps), theirs)

    def on_root(root):
        return root // NC == batch_pos // NC

    def after(array, earlier):
        return lax.optimization_barrier((array, earlier))[0]

    def both(*arrays):
        return lax.optimization_barrier(arrays)

    early = both(*[swapped[k] for k in range(far, 0, -1)])
    swapped.update(zip(range(far, 0, -1), early))
    give_own = inject(root_own, far, swapped[far])

    def energies(earlier):
        occ, virt, pairs, pairs_other, holds, _ = both(
            occ_energy, virt_energy, pair_list, pair_list_other, owned_occ, earlier
        )
        pairs = jnp.concatenate(
            [lax.dynamic_index_in_dim(p, core, 0) for p in (pairs, pairs_other)]
        )
        occ_sum = occ[pairs[:, 0]] + occ[pairs[:, 1]] + occ[holds[root_own]]
        energy_b = lax.dynamic_slice_in_dim(virt, slab_pos * local_b, local_b)
        energy_c = virt[:window]
        base = ((occ_sum[:, None, None] - energy_c) - energy_b[:, None]).reshape(2, n_rows)
        last = (NZ - 1) * piece
        spare = NZ * piece - n_rows
        base = jnp.concatenate(
            [base[:, :last], jnp.full((2, spare), 1e30, jnp.float32), base[:, last:]], axis=1
        ).reshape(2, NZ, piece)
        base = lax.dynamic_slice_in_dim(jnp.concatenate([base, base], axis=1), z, NZ, axis=1)
        base = jnp.where(up, jnp.roll(base[:, ::-1], 1, axis=1), base)
        ea = virt.reshape(NX, NYL, local_b)
        ea = jnp.where(yl == 0, ea, ea[:, ::-1])
        ea = lax.dynamic_slice_in_dim(jnp.concatenate([ea, ea], axis=0), x, NX, axis=0)
        ea = jnp.stack([ea, ea], axis=1).reshape(NX * 2 * NYL * local_b, 1)
        return base, ea

    got_own = send(give_own, Z_RING)
    give_other = got_other = None
    for k in range(far - 1, 0, -1):
        if give_other is not None:
            got_own = after(got_own, give_other)
        if k == far - 1:
            got_own, lam = both(got_own, lam)
            lam_up, lam_down = send(lam, x_by(-1)), send(lam, x_by(1))
        elif k == far - 2:
            got_other, lam_up, lam_down = both(got_other, lam_up, lam_down)
            lam_far = [send(lam_up[: NYL * local_b], x_by(-1))]
            lam_far.append(send(lam_down[NYL * local_b :], x_by(1)))
        give_own = jnp.where(on_root(root_own), inject(root_own, k, swapped[k]), got_own)
        got_own = send(give_own, Z_RING)
        if got_other is None:
            give_other = inject(root_other, k, after(swapped[k], give_own))
        else:
            got_other = after(got_other, give_own)
            give_other = jnp.where(
                on_root(root_other), inject(root_other, k, swapped[k]), got_other
            )
        got_other = send(give_other, Z_RING)
    base, ea = energies(got_own)
    got_other, _, base, ea, *lam_far = both(got_other, got_own, base, ea, *lam_far)
    crossed = send(got_other, SWAP_CORE)
    along = ((z - root_own // (NC * NYH)) * ahead_sign) % NZ
    mine = jnp.where(
        on_root(root_own),
        inject(root_own, 0, swapped[0]),
        jnp.where(along <= far, got_own, crossed),
    )
    here = jnp.where((root_own // NC) % NYH == yh, mine, send(mine, SWAP_YH))

    lams = []
    for rows in (lam, lam_up, lam_far, lam_down):
        if rows is not lam_far:
            rows = [rows[: NYL * local_b], rows[NYL * local_b :]]
        first, second = both(*rows, mine)[:2]
        got = send(jnp.where(up, second, first), SWAP_CORE)
        lams.append(jnp.concatenate([jnp.where(up, first, second), got]))

    here, *lams = both(here, *lams)
    ring_own, ring_other, crossed = [here], [send(here, SWAP_CORE)], [here]

    def base_of(order):
        return jnp.concatenate([base[:, k] for k in order], axis=1)

    total, lam = triples_call(base_of([0]), ea, lams, None, [here])
    for k in range(1, far):
        if k == 2:
            ring_own[-1], total = both(ring_own[-1], total)
        ring_own.append(send(ring_own[-1], Z_RING))
        if k == 3:
            first = [after(ring_own[1], ring_own[2]), crossed[1]]
            (total,) = triples_call(base_of([1, 7]), ea, lam, total, first)
            ring_other[-1], total = both(ring_other[-1], total)
            crossed.append(send(ring_other[-1], SWAP_CORE))
        ring_other.append(send(after(ring_other[-1], ring_own[k - 1]), Z_RING))
        if k == 1:
            crossed.append(send(ring_other[-1], SWAP_CORE))
    farthest = send(ring_own[-1], Z_RING)
    middle = [after(ring_own[2], ring_own[3]), crossed[2]]
    (total,) = triples_call(base_of([2, 6]), ea, lam, total, middle)
    late = [ring_own[3], send(after(ring_other[3], total), SWAP_CORE), farthest]
    kept, *by_x, kept_y, by_y = triples_call(base_of([3, 5, 4]), ea, lam, total, late, last=True)

    got_y = send(by_y, SWAP_YL)
    got_x = [send(by_x[step - 1], x_by(step)) for step in (2, 1, 3)]
    other, *coded = recode(kept_y, got_y)
    own = kept + sum(decode(got, width) for got in got_x)
    own = own[:local_b] + send(own[local_b:], SWAP_YL)
    got_x = [send(coded[step - 1], x_by(step)) for step in (2, 1, 3)]
    other = send(other + sum(decode(got, width) for got in got_x), SWAP_CORE)
    return jnp.where(up, jnp.stack([own, other]), jnp.stack([other, own]))


def solution(mesh):
    placed = (
        P("batch", "slab", None),
        P("batch", "slab", None),
        P("batch", None),
        P(),
        P(),
        P(),
        P(),
    )
    return jax.shard_map(
        body, mesh=mesh, in_specs=placed, out_specs=P("batch", "slab", None), check_vma=False
    )
```

```python
import functools

import jax
import jax.numpy as jnp
from jax import lax
from jax.experimental import pallas as pl
from jax.experimental.pallas import tpu as pltpu
from jax.sharding import PartitionSpec as P

AXES = ("batch", "slab")
NZ, NYH, NC, NX, NYL = 8, 2, 2, 4, 2


def full_perm(move):
    pairs = []
    for device in range(NZ * NYH * NC * NX * NYL):
        rest, yl = divmod(device, NYL)
        rest, x = divmod(rest, NX)
        rest, core = divmod(rest, NC)
        z, yh = divmod(rest, NYH)
        z, yh, core, x, yl = move(z, yh, core, x, yl)
        target = (((z % NZ) * NYH + yh % NYH) * NC + core % NC) * NX + x % NX
        pairs.append((device, target * NYL + yl % NYL))
    return pairs


SWAP_CORE = full_perm(lambda z, h, c, x, l: (z, h, 1 - c, x, l))
SWAP_YH = full_perm(lambda z, h, c, x, l: (z, 1 - h, c, x, l))
SWAP_YL = full_perm(lambda z, h, c, x, l: (z, h, c, x, 1 - l))
Z_RING = full_perm(lambda z, h, c, x, l: (z + 1 - 2 * c, h, c, x, l))


def x_by(step):
    return full_perm(lambda z, h, c, x, l: (z, h, c, x + step, l))


def send(array, perm):
    return lax.ppermute(array, AXES, perm)


def encode(value, wide):
    top = jnp.maximum(jnp.max(jnp.abs(value), axis=1, keepdims=True), 2.0**-110)
    exponent = jnp.ceil(jnp.log(top * 1.0001) * 1.4426950408889634) - 15.0
    coded = jnp.floor(value * jnp.exp2(-exponent) + 0.5)
    tail = jnp.broadcast_to(exponent, (value.shape[0], wide - value.shape[1]))
    return jnp.concatenate([coded, tail], axis=1).astype(jnp.int32).astype(jnp.int16)


def decode(coded, width):
    coded = coded.astype(jnp.float32)
    return coded[:, :width] * jnp.exp2(coded[:, width : width + 1])


def triples_kernel(n_pieces, first, last, chunk, *refs):
    base_ref, ea_ref = refs[:2]
    if first:
        lam_refs = refs[2 : 2 + NX]
        at = 2 + NX
    else:
        lam_ref, prev_ref = refs[2:4]
        at = 4
    pieces = refs[at : at + n_pieces]
    outs = refs[at + n_pieces : len(refs) - 1]
    block_ref = refs[-1]
    g = pl.program_id(0)

    @pl.when(g == 0)
    def _():
        to = 0
        for piece in pieces:
            rows = piece.shape[0]
            block_ref[to : to + rows, :] = piece[...]
            to += rows

    if last:
        kept_ref, *by_x_refs, kept_y_ref, by_y_ref, total_ref = outs
    elif not first:
        (total_ref,) = outs
    else:
        total_ref, lam_ref = outs
        for k in range(NX):

            @pl.when(g == k)
            def _():
                lam_ref[...] = lam_refs[k][...]

    lam = lam_ref[...]
    part = lam.shape[0] // 2
    rows = block_ref.shape[0]
    for at in range(0, rows, chunk):
        size = min(chunk, rows - at)
        block = block_ref[at : at + size, :]
        weighted = lax.dot_general(
            lam, block, (((1,), (1,)), ((), ())), preferred_element_type=jnp.float32
        )
        divided = []
        for k in range(2):
            denom = base_ref[k : k + 1, at : at + size] - ea_ref[k * part : (k + 1) * part, :]
            inverse = pl.reciprocal(denom, approx=True)
            inverse = inverse * (2.0 - denom * inverse)
            divided.append(weighted[k * part : (k + 1) * part] * inverse)
        triples = jnp.concatenate(divided, axis=0).astype(jnp.bfloat16)
        share = jnp.dot(triples, block, preferred_element_type=jnp.float32)
        if at:
            total_ref[...] += share
        elif first:
            total_ref[...] = share
        else:
            total_ref[...] = prev_ref[...] + share
    if not last:
        return
    wide = by_y_ref.shape[2]
    mid = part + part // 2

    @pl.when(g == 0)
    def _():
        kept_ref[...] = total_ref[:part, :]

    for k in range(1, NX):

        @pl.when(g == k)
        def _():
            by_x_refs[k - 1][...] = encode(total_ref[:part, :], wide)

    kept_y_ref[0] = total_ref[part:mid, :]
    by_y_ref[0] = encode(total_ref[mid:, :], wide)


def whole(shape):
    return pl.BlockSpec(shape, lambda g: (0,) * len(shape))


def held(shape):
    return pl.BlockSpec(shape, lambda g: (0,) * len(shape), pipeline_mode=pl.Buffered(1))


def by_step(shape):
    return pl.BlockSpec((1,) + shape[1:], lambda g: (g, 0, 0))


def triples_call(base, ea, lams, prev, pieces, last=False):
    first = prev is None
    rows = sum(p.shape[0] for p in pieces)
    tile, width = lams[0].shape if first else (lams.shape[0] // NX, lams.shape[1])
    padded = -(-rows // 128) * 128
    base = jnp.pad(base, ((0, 0), (0, padded - rows)), constant_values=1.0)
    spec = pl.BlockSpec((tile, width), lambda g: (g, 0))
    in_specs = [held(base.shape), pl.BlockSpec((tile, 1), lambda g: (g, 0))]
    in_specs += [held(p.shape) for p in lams] if first else [spec, spec]
    in_specs += [held(p.shape) for p in pieces]
    args = [base, ea, *(lams if first else [lams, prev]), *pieces]
    scratch = [pltpu.VMEM((rows, width), jnp.bfloat16)]
    if last:
        half = tile // 2
        wide = -(-(width + 1) // 128) * 128
        shapes = [((half, width), jnp.float32)] + [((half, wide), jnp.int16)] * (NX - 1)
        out_specs = [whole(shape) for shape, _ in shapes]
        pair = [((NX, half // 2, width), jnp.float32), ((NX, half // 2, wide), jnp.int16)]
        out_specs += [by_step(shape) for shape, _ in pair]
        shapes += pair
        scratch = [pltpu.VMEM((tile, width), jnp.float32)] + scratch
    else:
        shapes = [((NX * tile, width), jnp.float32), ((NX * tile, width), jnp.bfloat16)]
        shapes = shapes[: 1 + first]
        out_specs = [spec] * len(shapes)
    return pl.pallas_call(
        functools.partial(triples_kernel, len(pieces), first, last, 1024),
        grid=(NX,),
        in_specs=in_specs,
        out_specs=out_specs,
        out_shape=[jax.ShapeDtypeStruct(*shape) for shape in shapes],
        scratch_shapes=scratch,
        compiler_params=pltpu.CompilerParams(vmem_limit_bytes=26 * 1024 * 1024),
        cost_estimate=pl.CostEstimate(
            flops=4 * rows * NX * tile * width,
            bytes_accessed=2 * rows * width + 10 * NX * tile * width,
            transcendentals=0,
        ),
    )(*args)


def recode_kernel(kept_ref, got_ref, own_ref, *coded_refs):
    g = pl.program_id(0)
    total = kept_ref[0] + decode(got_ref[0], kept_ref.shape[2])

    @pl.when(g == 0)
    def _():
        own_ref[...] = total

    for k in range(1, NX):

        @pl.when(g == k)
        def _():
            coded_refs[k - 1][...] = encode(total, got_ref.shape[2])


def recode(kept, got):
    shapes = [(kept.shape[1:], jnp.float32)] + [(got.shape[1:], jnp.int16)] * (NX - 1)
    return pl.pallas_call(
        recode_kernel,
        grid=(NX,),
        in_specs=[by_step(kept.shape), by_step(got.shape)],
        out_specs=[whole(shape) for shape, _ in shapes],
        out_shape=[jax.ShapeDtypeStruct(*shape) for shape in shapes],
        compiler_params=pltpu.CompilerParams(vmem_limit_bytes=16 * 1024 * 1024),
        cost_estimate=pl.CostEstimate(
            flops=10 * kept.size, bytes_accessed=10 * kept.size, transcendentals=0
        ),
    )(kept, got)


def body(lambda_pairs, vvvo, pair_list, owned_occ, step_root, occ_energy, virt_energy):
    window, local_b, width = vvvo.shape
    n_rows = window * local_b
    batch_pos = lax.axis_index("batch")
    slab_pos = lax.axis_index("slab")
    core = batch_pos % NC
    yh = (batch_pos // NC) % NYH
    z = batch_pos // (NC * NYH)
    x = slab_pos // NYL
    yl = slab_pos % NYL
    up = core == 0
    ahead_sign = 1 - 2 * core
    root_own = jnp.where(up, step_root[0], step_root[1])
    root_other = jnp.where(up, step_root[1], step_root[0])

    pair_list_other = send(pair_list, SWAP_CORE)

    lam = jnp.stack([lambda_pairs, send(lambda_pairs, SWAP_YL)], axis=1)
    lam = lam.reshape(2 * NYL * local_b, width)

    flat = vvvo.transpose(1, 0, 2).reshape(n_rows, width)
    far = NZ // 2

    piece = -(-n_rows // (NZ * 16)) * 16

    def ahead(sign, steps, rows=flat):
        start = jnp.minimum((z + sign * steps) % NZ * piece, n_rows - piece)
        return lax.dynamic_slice_in_dim(rows, start, piece)

    swapped = {k: send(ahead(-ahead_sign, k), SWAP_CORE) for k in (far, far - 1)}

    def inject(root, steps, theirs):
        return jnp.where(root % NC == core, ahead(ahead_sign, steps), theirs)

    def on_root(root):
        return root // NC == batch_pos // NC

    def after(array, earlier):
        return lax.optimization_barrier((array, earlier))[0]

    def both(*arrays):
        return lax.optimization_barrier(arrays)

    swapped[far], swapped[far - 1] = both(swapped[far], swapped[far - 1])
    give_own = inject(root_own, far, swapped[far])
    flat_later = after(flat, give_own)
    for k in range(far - 2, -1, -1):
        swapped[k] = send(ahead(-ahead_sign, k, flat_later), SWAP_CORE)

    def energies(earlier):
        occ, virt, pairs, pairs_other, holds, _ = both(
            occ_energy, virt_energy, pair_list, pair_list_other, owned_occ, earlier
        )
        pairs = jnp.concatenate(
            [lax.dynamic_index_in_dim(p, core, 0) for p in (pairs, pairs_other)]
        )
        occ_sum = occ[pairs[:, 0]] + occ[pairs[:, 1]] + occ[holds[root_own]]
        energy_b = lax.dynamic_slice_in_dim(virt, slab_pos * local_b, local_b)
        energy_c = virt[:window]
        base = ((occ_sum[:, None, None] - energy_c) - energy_b[:, None]).reshape(2, n_rows)
        last = (NZ - 1) * piece
        spare = NZ * piece - n_rows
        base = jnp.concatenate(
            [base[:, :last], jnp.full((2, spare), 1e30, jnp.float32), base[:, last:]], axis=1
        ).reshape(2, NZ, piece)
        base = lax.dynamic_slice_in_dim(jnp.concatenate([base, base], axis=1), z, NZ, axis=1)
        base = jnp.where(up, jnp.roll(base[:, ::-1], 1, axis=1), base)
        ea = virt.reshape(NX, NYL, local_b)
        ea = jnp.where(yl == 0, ea, ea[:, ::-1])
        ea = lax.dynamic_slice_in_dim(jnp.concatenate([ea, ea], axis=0), x, NX, axis=0)
        ea = jnp.stack([ea, ea], axis=1).reshape(NX * 2 * NYL * local_b, 1)
        return base, ea

    got_own = send(give_own, Z_RING)
    give_other = got_other = None
    for k in range(far - 1, 0, -1):
        if give_other is not None:
            got_own = after(got_own, give_other)
        if k == far - 1:
            got_own, swapped[2], swapped[1] = both(got_own, swapped[2], swapped[1])
        elif k == far - 2:
            got_other, lam_up, lam_down = both(got_other, lam_up, lam_down)
            lam_far = [send(lam_up[: NYL * local_b], x_by(-1))]
            lam_far.append(send(lam_down[NYL * local_b :], x_by(1)))
        give_own = jnp.where(on_root(root_own), inject(root_own, k, swapped[k]), got_own)
        got_own = send(give_own, Z_RING)
        if got_other is None:
            theirs, _, lam = both(swapped[k], give_own, lam)
            lam_up, lam_down = send(lam, x_by(-1)), send(lam, x_by(1))
            give_other = inject(root_other, k, theirs)
        else:
            got_other = after(got_other, give_own)
            give_other = jnp.where(
                on_root(root_other), inject(root_other, k, swapped[k]), got_other
            )
        got_other = send(give_other, Z_RING)
    base, ea = energies(got_own)
    got_other, _, base, ea, *lam_far = both(got_other, got_own, base, ea, *lam_far)
    crossed = send(got_other, SWAP_CORE)
    along = ((z - root_own // (NC * NYH)) * ahead_sign) % NZ
    mine = jnp.where(
        on_root(root_own),
        inject(root_own, 0, swapped[0]),
        jnp.where(along <= far, got_own, crossed),
    )
    here = jnp.where((root_own // NC) % NYH == yh, mine, send(mine, SWAP_YH))

    lams = []
    for rows in (lam, lam_up, lam_far, lam_down):
        if rows is not lam_far:
            rows = [rows[: NYL * local_b], rows[NYL * local_b :]]
        first, second = both(*rows, mine)[:2]
        got = send(jnp.where(up, second, first), SWAP_CORE)
        lams.append(jnp.concatenate([jnp.where(up, first, second), got]))

    here, *lams = both(here, *lams)
    ring_own, ring_other, crossed = [here], [send(here, SWAP_CORE)], [here]

    def base_of(order):
        return jnp.concatenate([base[:, k] for k in order], axis=1)

    total, lam = triples_call(base_of([0]), ea, lams, None, [here])
    for k in range(1, far):
        if k == 2:
            ring_own[-1], total = both(ring_own[-1], total)
        ring_own.append(send(ring_own[-1], Z_RING))
        if k == 3:
            first = [after(ring_own[1], ring_own[2]), crossed[1]]
            (total,) = triples_call(base_of([1, 7]), ea, lam, total, first)
            ring_other[-1], total = both(ring_other[-1], total)
            crossed.append(send(ring_other[-1], SWAP_CORE))
        ring_other.append(send(after(ring_other[-1], ring_own[k - 1]), Z_RING))
        if k == 1:
            crossed.append(send(ring_other[-1], SWAP_CORE))
    farthest = send(ring_own[-1], Z_RING)
    middle = [after(ring_own[2], ring_own[3]), crossed[2]]
    (total,) = triples_call(base_of([2, 6]), ea, lam, total, middle)
    late = [ring_own[3], send(after(ring_other[3], total), SWAP_CORE), farthest]
    kept, *by_x, kept_y, by_y = triples_call(base_of([3, 5, 4]), ea, lam, total, late, last=True)

    got_y = send(by_y, SWAP_YL)
    got_x = [send(by_x[step - 1], x_by(step)) for step in (2, 1, 3)]
    other, *coded = recode(kept_y, got_y)
    own = kept + sum(decode(got, width) for got in got_x)
    own = own[:local_b] + send(own[local_b:], SWAP_YL)
    got_x = [send(coded[step - 1], x_by(step)) for step in (2, 1, 3)]
    other = send(other + sum(decode(got, width) for got in got_x), SWAP_CORE)
    return jnp.where(up, jnp.stack([own, other]), jnp.stack([other, own]))


def solution(mesh):
    placed = (
        P("batch", "slab", None),
        P("batch", "slab", None),
        P("batch", None),
        P(),
        P(),
        P(),
        P(),
    )
    return jax.shard_map(
        body, mesh=mesh, in_specs=placed, out_specs=P("batch", "slab", None), check_vma=False
    )
```

```python
import functools

import jax
import jax.numpy as jnp
from jax import lax
from jax.experimental import pallas as pl
from jax.experimental.pallas import tpu as pltpu
from jax.sharding import PartitionSpec as P

AXES = ("batch", "slab")
NZ, NYH, NC, NX, NYL = 8, 2, 2, 4, 2


def full_perm(move):
    pairs = []
    for device in range(NZ * NYH * NC * NX * NYL):
        rest, yl = divmod(device, NYL)
        rest, x = divmod(rest, NX)
        rest, core = divmod(rest, NC)
        z, yh = divmod(rest, NYH)
        z, yh, core, x, yl = move(z, yh, core, x, yl)
        target = (((z % NZ) * NYH + yh % NYH) * NC + core % NC) * NX + x % NX
        pairs.append((device, target * NYL + yl % NYL))
    return pairs


SWAP_CORE = full_perm(lambda z, h, c, x, l: (z, h, 1 - c, x, l))
SWAP_YH = full_perm(lambda z, h, c, x, l: (z, 1 - h, c, x, l))
SWAP_YL = full_perm(lambda z, h, c, x, l: (z, h, c, x, 1 - l))
Z_RING = full_perm(lambda z, h, c, x, l: (z + 1 - 2 * c, h, c, x, l))


def x_by(step):
    return full_perm(lambda z, h, c, x, l: (z, h, c, x + step, l))


def send(array, perm):
    return lax.ppermute(array, AXES, perm)


def encode(value, wide):
    top = jnp.maximum(jnp.max(jnp.abs(value), axis=1, keepdims=True), 2.0**-110)
    exponent = jnp.ceil(jnp.log(top * 1.0001) * 1.4426950408889634) - 15.0
    coded = jnp.floor(value * jnp.exp2(-exponent) + 0.5)
    tail = jnp.broadcast_to(exponent, (value.shape[0], wide - value.shape[1]))
    return jnp.concatenate([coded, tail], axis=1).astype(jnp.int32).astype(jnp.int16)


def decode(coded, width):
    coded = coded.astype(jnp.float32)
    return coded[:, :width] * jnp.exp2(coded[:, width : width + 1])


def triples_kernel(n_pieces, first, last, chunk, *refs):
    base_ref, ea_ref = refs[:2]
    if first:
        lam_refs = refs[2 : 2 + NX]
        at = 2 + NX
    else:
        lam_ref, prev_ref = refs[2:4]
        at = 4
    pieces = refs[at : at + n_pieces]
    outs = refs[at + n_pieces : len(refs) - 1]
    block_ref = refs[-1]
    g = pl.program_id(0)

    @pl.when(g == 0)
    def _():
        to = 0
        for piece in pieces:
            rows = piece.shape[0]
            block_ref[to : to + rows, :] = piece[...]
            to += rows

    if last:
        kept_ref, *by_x_refs, kept_y_ref, by_y_ref, total_ref = outs
    elif not first:
        (total_ref,) = outs
    else:
        total_ref, lam_ref = outs
        for k in range(NX):

            @pl.when(g == k)
            def _():
                lam_ref[...] = lam_refs[k][...]

    lam = lam_ref[...]
    part = lam.shape[0] // 2
    rows = block_ref.shape[0]
    for at in range(0, rows, chunk):
        size = min(chunk, rows - at)
        block = block_ref[at : at + size, :]
        weighted = lax.dot_general(
            lam, block, (((1,), (1,)), ((), ())), preferred_element_type=jnp.float32
        )
        divided = []
        for k in range(2):
            denom = base_ref[k : k + 1, at : at + size] - ea_ref[k * part : (k + 1) * part, :]
            inverse = pl.reciprocal(denom, approx=True)
            inverse = inverse * (2.0 - denom * inverse)
            divided.append(weighted[k * part : (k + 1) * part] * inverse)
        triples = jnp.concatenate(divided, axis=0).astype(jnp.bfloat16)
        share = jnp.dot(triples, block, preferred_element_type=jnp.float32)
        if at:
            total_ref[...] += share
        elif first:
            total_ref[...] = share
        else:
            total_ref[...] = prev_ref[...] + share
    if not last:
        return
    wide = by_y_ref.shape[2]
    mid = part + part // 2

    @pl.when(g == 0)
    def _():
        kept_ref[...] = total_ref[:part, :]

    for k in range(1, NX):

        @pl.when(g == k)
        def _():
            by_x_refs[k - 1][...] = encode(total_ref[:part, :], wide)

    kept_y_ref[0] = total_ref[part:mid, :]
    by_y_ref[0] = encode(total_ref[mid:, :], wide)


def whole(shape):
    return pl.BlockSpec(shape, lambda g: (0,) * len(shape))


def held(shape):
    return pl.BlockSpec(shape, lambda g: (0,) * len(shape), pipeline_mode=pl.Buffered(1))


def by_step(shape):
    return pl.BlockSpec((1,) + shape[1:], lambda g: (g, 0, 0))


def triples_call(base, ea, lams, prev, pieces, last=False):
    first = prev is None
    rows = sum(p.shape[0] for p in pieces)
    tile, width = lams[0].shape if first else (lams.shape[0] // NX, lams.shape[1])
    padded = -(-rows // 128) * 128
    base = jnp.pad(base, ((0, 0), (0, padded - rows)), constant_values=1.0)
    spec = pl.BlockSpec((tile, width), lambda g: (g, 0))
    in_specs = [held(base.shape), pl.BlockSpec((tile, 1), lambda g: (g, 0))]
    in_specs += [held(p.shape) for p in lams] if first else [spec, spec]
    in_specs += [held(p.shape) for p in pieces]
    args = [base, ea, *(lams if first else [lams, prev]), *pieces]
    scratch = [pltpu.VMEM((rows, width), jnp.bfloat16)]
    if last:
        half = tile // 2
        wide = -(-(width + 1) // 128) * 128
        shapes = [((half, width), jnp.float32)] + [((half, wide), jnp.int16)] * (NX - 1)
        out_specs = [whole(shape) for shape, _ in shapes]
        pair = [((NX, half // 2, width), jnp.float32), ((NX, half // 2, wide), jnp.int16)]
        out_specs += [by_step(shape) for shape, _ in pair]
        shapes += pair
        scratch = [pltpu.VMEM((tile, width), jnp.float32)] + scratch
    else:
        shapes = [((NX * tile, width), jnp.float32), ((NX * tile, width), jnp.bfloat16)]
        shapes = shapes[: 1 + first]
        out_specs = [spec] * len(shapes)
    return pl.pallas_call(
        functools.partial(triples_kernel, len(pieces), first, last, 1024),
        grid=(NX,),
        in_specs=in_specs,
        out_specs=out_specs,
        out_shape=[jax.ShapeDtypeStruct(*shape) for shape in shapes],
        scratch_shapes=scratch,
        compiler_params=pltpu.CompilerParams(vmem_limit_bytes=26 * 1024 * 1024),
        cost_estimate=pl.CostEstimate(
            flops=4 * rows * NX * tile * width,
            bytes_accessed=2 * rows * width + 10 * NX * tile * width,
            transcendentals=0,
        ),
    )(*args)


def recode_kernel(kept_ref, got_ref, own_ref, *coded_refs):
    g = pl.program_id(0)
    total = kept_ref[0] + decode(got_ref[0], kept_ref.shape[2])

    @pl.when(g == 0)
    def _():
        own_ref[...] = total

    for k in range(1, NX):

        @pl.when(g == k)
        def _():
            coded_refs[k - 1][...] = encode(total, got_ref.shape[2])


def recode(kept, got):
    shapes = [(kept.shape[1:], jnp.float32)] + [(got.shape[1:], jnp.int16)] * (NX - 1)
    return pl.pallas_call(
        recode_kernel,
        grid=(NX,),
        in_specs=[by_step(kept.shape), by_step(got.shape)],
        out_specs=[whole(shape) for shape, _ in shapes],
        out_shape=[jax.ShapeDtypeStruct(*shape) for shape in shapes],
        compiler_params=pltpu.CompilerParams(vmem_limit_bytes=16 * 1024 * 1024),
        cost_estimate=pl.CostEstimate(
            flops=10 * kept.size, bytes_accessed=10 * kept.size, transcendentals=0
        ),
    )(kept, got)


def body(lambda_pairs, vvvo, pair_list, owned_occ, step_root, occ_energy, virt_energy):
    window, local_b, width = vvvo.shape
    n_rows = window * local_b
    batch_pos = lax.axis_index("batch")
    slab_pos = lax.axis_index("slab")
    core = batch_pos % NC
    yh = (batch_pos // NC) % NYH
    z = batch_pos // (NC * NYH)
    x = slab_pos // NYL
    yl = slab_pos % NYL
    up = core == 0
    ahead_sign = 1 - 2 * core
    root_own = jnp.where(up, step_root[0], step_root[1])
    root_other = jnp.where(up, step_root[1], step_root[0])

    pair_list_other = send(pair_list, SWAP_CORE)

    lam = jnp.stack([lambda_pairs, send(lambda_pairs, SWAP_YL)], axis=1)
    lam = lam.reshape(2 * NYL * local_b, width)

    flat = vvvo.transpose(1, 0, 2).reshape(n_rows, width)
    far = NZ // 2

    piece = -(-n_rows // (NZ * 16)) * 16

    def ahead(sign, steps, rows=flat):
        start = jnp.minimum((z + sign * steps) % NZ * piece, n_rows - piece)
        return lax.dynamic_slice_in_dim(rows, start, piece)

    swapped = {k: send(ahead(-ahead_sign, k), SWAP_CORE) for k in (far, far - 1)}

    def inject(root, steps, theirs):
        return jnp.where(root % NC == core, ahead(ahead_sign, steps), theirs)

    def on_root(root):
        return root // NC == batch_pos // NC

    def after(array, earlier):
        return lax.optimization_barrier((array, earlier))[0]

    def both(*arrays):
        return lax.optimization_barrier(arrays)

    swapped[far], swapped[far - 1], pair_list_other = both(
        swapped[far], swapped[far - 1], pair_list_other
    )
    give_own = inject(root_own, far, swapped[far])
    flat_later = after(flat, give_own)
    for k in range(far - 2, 0, -1):
        swapped[k] = send(ahead(-ahead_sign, k, flat_later), SWAP_CORE)

    def energies(earlier):
        occ, virt, pairs, pairs_other, holds, _ = both(
            occ_energy, virt_energy, pair_list, pair_list_other, owned_occ, earlier
        )
        pairs = jnp.concatenate(
            [lax.dynamic_index_in_dim(p, core, 0) for p in (pairs, pairs_other)]
        )
        occ_sum = occ[pairs[:, 0]] + occ[pairs[:, 1]] + occ[holds[root_own]]
        energy_b = lax.dynamic_slice_in_dim(virt, slab_pos * local_b, local_b)
        energy_c = virt[:window]
        base = ((occ_sum[:, None, None] - energy_c) - energy_b[:, None]).reshape(2, n_rows)
        last = (NZ - 1) * piece
        spare = NZ * piece - n_rows
        base = jnp.concatenate(
            [base[:, :last], jnp.full((2, spare), 1e30, jnp.float32), base[:, last:]], axis=1
        ).reshape(2, NZ, piece)
        base = lax.dynamic_slice_in_dim(jnp.concatenate([base, base], axis=1), z, NZ, axis=1)
        base = jnp.where(up, jnp.roll(base[:, ::-1], 1, axis=1), base)
        ea = virt.reshape(NX, NYL, local_b)
        ea = jnp.where(yl == 0, ea, ea[:, ::-1])
        ea = lax.dynamic_slice_in_dim(jnp.concatenate([ea, ea], axis=0), x, NX, axis=0)
        ea = jnp.stack([ea, ea], axis=1).reshape(NX * 2 * NYL * local_b, 1)
        return base, ea

    got_own = send(give_own, Z_RING)
    give_other = got_other = None
    for k in range(far - 1, 0, -1):
        if give_other is not None:
            got_own = after(got_own, give_other)
        if k == far - 1:
            got_own, swapped[2], swapped[1] = both(got_own, swapped[2], swapped[1])
        elif k == far - 2:
            got_other, lam_up, lam_down = both(got_other, lam_up, lam_down)
            lam_far = [send(lam_up[: NYL * local_b], x_by(-1))]
            lam_far.append(send(lam_down[NYL * local_b :], x_by(1)))
        give_own = jnp.where(on_root(root_own), inject(root_own, k, swapped[k]), got_own)
        got_own = send(give_own, Z_RING)
        if got_other is None:
            theirs, _, lam = both(swapped[k], give_own, lam)
            lam_up, lam_down = send(lam, x_by(-1)), send(lam, x_by(1))
            give_other = inject(root_other, k, theirs)
        else:
            got_other = after(got_other, give_own)
            give_other = jnp.where(
                on_root(root_other), inject(root_other, k, swapped[k]), got_other
            )
        got_other = send(give_other, Z_RING)
    swapped[0] = send(ahead(-ahead_sign, 0, after(flat, give_other)), SWAP_CORE)
    base, ea = energies(got_own)
    got_other, _, base, ea, *lam_far = both(got_other, got_own, base, ea, *lam_far)
    crossed = send(got_other, SWAP_CORE)
    along = ((z - root_own // (NC * NYH)) * ahead_sign) % NZ
    mine = jnp.where(
        on_root(root_own),
        inject(root_own, 0, swapped[0]),
        jnp.where(along <= far, got_own, crossed),
    )
    here = jnp.where((root_own // NC) % NYH == yh, mine, send(mine, SWAP_YH))

    lams = []
    for rows in (lam, lam_up, lam_far, lam_down):
        if rows is not lam_far:
            rows = [rows[: NYL * local_b], rows[NYL * local_b :]]
        first, second = both(*rows, mine)[:2]
        got = send(jnp.where(up, second, first), SWAP_CORE)
        lams.append(jnp.concatenate([jnp.where(up, first, second), got]))

    here, *lams = both(here, *lams)
    ring_own, ring_other, crossed = [here], [send(here, SWAP_CORE)], [here]

    def base_of(order):
        return jnp.concatenate([base[:, k] for k in order], axis=1)

    total, lam = triples_call(base_of([0]), ea, lams, None, [here])
    for k in range(1, far):
        if k == 2:
            ring_own[-1], total = both(ring_own[-1], total)
        ring_own.append(send(ring_own[-1], Z_RING))
        if k == 3:
            first = [after(ring_own[1], ring_own[2]), crossed[1]]
            (total,) = triples_call(base_of([1, 7]), ea, lam, total, first)
            ring_other[-1], total = both(ring_other[-1], total)
            crossed.append(send(ring_other[-1], SWAP_CORE))
        ring_other.append(send(after(ring_other[-1], ring_own[k - 1]), Z_RING))
        if k == 1:
            crossed.append(send(ring_other[-1], SWAP_CORE))
    farthest = send(ring_own[-1], Z_RING)
    middle = [after(ring_own[2], ring_own[3]), crossed[2]]
    (total,) = triples_call(base_of([2, 6]), ea, lam, total, middle)
    late = [ring_own[3], send(after(ring_other[3], total), SWAP_CORE), farthest]
    kept, *by_x, kept_y, by_y = triples_call(base_of([3, 5, 4]), ea, lam, total, late, last=True)

    got_y = send(by_y, SWAP_YL)
    got_x = [send(by_x[step - 1], x_by(step)) for step in (2, 1, 3)]
    other, *coded = recode(kept_y, got_y)
    own = kept + sum(decode(got, width) for got in got_x)
    own = own[:local_b] + send(own[local_b:], SWAP_YL)
    got_x = [send(coded[step - 1], x_by(step)) for step in (2, 1, 3)]
    other = send(other + sum(decode(got, width) for got in got_x), SWAP_CORE)
    return jnp.where(up, jnp.stack([own, other]), jnp.stack([other, own]))


def solution(mesh):
    placed = (
        P("batch", "slab", None),
        P("batch", "slab", None),
        P("batch", None),
        P(),
        P(),
        P(),
        P(),
    )
    return jax.shard_map(
        body, mesh=mesh, in_specs=placed, out_specs=P("batch", "slab", None), check_vma=False
    )
```

```python
import functools

import jax
import jax.numpy as jnp
from jax import lax
from jax.experimental import pallas as pl
from jax.experimental.pallas import tpu as pltpu
from jax.sharding import PartitionSpec as P

AXES = ("batch", "slab")
NZ, NYH, NC, NX, NYL = 8, 2, 2, 4, 2


def full_perm(move):
    pairs = []
    for device in range(NZ * NYH * NC * NX * NYL):
        rest, yl = divmod(device, NYL)
        rest, x = divmod(rest, NX)
        rest, core = divmod(rest, NC)
        z, yh = divmod(rest, NYH)
        z, yh, core, x, yl = move(z, yh, core, x, yl)
        target = (((z % NZ) * NYH + yh % NYH) * NC + core % NC) * NX + x % NX
        pairs.append((device, target * NYL + yl % NYL))
    return pairs


SWAP_CORE = full_perm(lambda z, h, c, x, l: (z, h, 1 - c, x, l))
SWAP_YH = full_perm(lambda z, h, c, x, l: (z, 1 - h, c, x, l))
SWAP_YL = full_perm(lambda z, h, c, x, l: (z, h, c, x, 1 - l))
Z_RING = full_perm(lambda z, h, c, x, l: (z + 1 - 2 * c, h, c, x, l))


def x_by(step):
    return full_perm(lambda z, h, c, x, l: (z, h, c, x + step, l))


def send(array, perm):
    return lax.ppermute(array, AXES, perm)


def encode(value, wide):
    top = jnp.maximum(jnp.max(jnp.abs(value), axis=1, keepdims=True), 2.0**-110)
    exponent = jnp.ceil(jnp.log(top * 1.0001) * 1.4426950408889634) - 15.0
    coded = jnp.floor(value * jnp.exp2(-exponent) + 0.5)
    tail = jnp.broadcast_to(exponent, (value.shape[0], wide - value.shape[1]))
    return jnp.concatenate([coded, tail], axis=1).astype(jnp.int32).astype(jnp.int16)


def decode(coded, width):
    coded = coded.astype(jnp.float32)
    return coded[:, :width] * jnp.exp2(coded[:, width : width + 1])


def triples_kernel(n_pieces, first, last, chunk, *refs):
    base_ref, ea_ref = refs[:2]
    if first:
        lam_refs = refs[2 : 2 + NX]
        at = 2 + NX
    else:
        lam_ref, prev_ref = refs[2:4]
        at = 4
    pieces = refs[at : at + n_pieces]
    outs = refs[at + n_pieces : len(refs) - 1]
    block_ref = refs[-1]
    g = pl.program_id(0)

    @pl.when(g == 0)
    def _():
        to = 0
        for piece in pieces:
            rows = piece.shape[0]
            block_ref[to : to + rows, :] = piece[...]
            to += rows

    if last:
        kept_ref, *by_x_refs, kept_y_ref, by_y_ref, total_ref = outs
    elif not first:
        (total_ref,) = outs
    else:
        total_ref, lam_ref = outs
        for k in range(NX):

            @pl.when(g == k)
            def _():
                lam_ref[...] = lam_refs[k][...]

    lam = lam_ref[...]
    part = lam.shape[0] // 2
    rows = block_ref.shape[0]
    for at in range(0, rows, chunk):
        size = min(chunk, rows - at)
        block = block_ref[at : at + size, :]
        weighted = lax.dot_general(
            lam, block, (((1,), (1,)), ((), ())), preferred_element_type=jnp.float32
        )
        divided = []
        for k in range(2):
            denom = base_ref[k : k + 1, at : at + size] - ea_ref[k * part : (k + 1) * part, :]
            inverse = pl.reciprocal(denom, approx=True)
            inverse = inverse * (2.0 - denom * inverse)
            divided.append(weighted[k * part : (k + 1) * part] * inverse)
        triples = jnp.concatenate(divided, axis=0).astype(jnp.bfloat16)
        share = jnp.dot(triples, block, preferred_element_type=jnp.float32)
        if at:
            total_ref[...] += share
        elif first:
            total_ref[...] = share
        else:
            total_ref[...] = prev_ref[...] + share
    if not last:
        return
    wide = by_y_ref.shape[2]
    mid = part + part // 2

    @pl.when(g == 0)
    def _():
        kept_ref[...] = total_ref[:part, :]

    for k in range(1, NX):

        @pl.when(g == k)
        def _():
            by_x_refs[k - 1][...] = encode(total_ref[:part, :], wide)

    kept_y_ref[0] = total_ref[part:mid, :]
    by_y_ref[0] = encode(total_ref[mid:, :], wide)


def whole(shape):
    return pl.BlockSpec(shape, lambda g: (0,) * len(shape))


def held(shape):
    return pl.BlockSpec(shape, lambda g: (0,) * len(shape), pipeline_mode=pl.Buffered(1))


def by_step(shape):
    return pl.BlockSpec((1,) + shape[1:], lambda g: (g, 0, 0))


def triples_call(base, ea, lams, prev, pieces, last=False):
    first = prev is None
    rows = sum(p.shape[0] for p in pieces)
    tile, width = lams[0].shape if first else (lams.shape[0] // NX, lams.shape[1])
    padded = -(-rows // 128) * 128
    base = jnp.pad(base, ((0, 0), (0, padded - rows)), constant_values=1.0)
    spec = pl.BlockSpec((tile, width), lambda g: (g, 0))
    in_specs = [held(base.shape), pl.BlockSpec((tile, 1), lambda g: (g, 0))]
    in_specs += [held(p.shape) for p in lams] if first else [spec, spec]
    in_specs += [held(p.shape) for p in pieces]
    args = [base, ea, *(lams if first else [lams, prev]), *pieces]
    scratch = [pltpu.VMEM((rows, width), jnp.bfloat16)]
    if last:
        half = tile // 2
        wide = -(-(width + 1) // 128) * 128
        shapes = [((half, width), jnp.float32)] + [((half, wide), jnp.int16)] * (NX - 1)
        out_specs = [whole(shape) for shape, _ in shapes]
        pair = [((NX, half // 2, width), jnp.float32), ((NX, half // 2, wide), jnp.int16)]
        out_specs += [by_step(shape) for shape, _ in pair]
        shapes += pair
        scratch = [pltpu.VMEM((tile, width), jnp.float32)] + scratch
    else:
        shapes = [((NX * tile, width), jnp.float32), ((NX * tile, width), jnp.bfloat16)]
        shapes = shapes[: 1 + first]
        out_specs = [spec] * len(shapes)
    return pl.pallas_call(
        functools.partial(triples_kernel, len(pieces), first, last, 1024),
        grid=(NX,),
        in_specs=in_specs,
        out_specs=out_specs,
        out_shape=[jax.ShapeDtypeStruct(*shape) for shape in shapes],
        scratch_shapes=scratch,
        compiler_params=pltpu.CompilerParams(vmem_limit_bytes=26 * 1024 * 1024),
        cost_estimate=pl.CostEstimate(
            flops=4 * rows * NX * tile * width,
            bytes_accessed=2 * rows * width + 10 * NX * tile * width,
            transcendentals=0,
        ),
    )(*args)


def recode_kernel(kept_ref, got_ref, own_ref, *coded_refs):
    g = pl.program_id(0)
    total = kept_ref[0] + decode(got_ref[0], kept_ref.shape[2])

    @pl.when(g == 0)
    def _():
        own_ref[...] = total

    for k in range(1, NX):

        @pl.when(g == k)
        def _():
            coded_refs[k - 1][...] = encode(total, got_ref.shape[2])


def recode(kept, got):
    shapes = [(kept.shape[1:], jnp.float32)] + [(got.shape[1:], jnp.int16)] * (NX - 1)
    return pl.pallas_call(
        recode_kernel,
        grid=(NX,),
        in_specs=[by_step(kept.shape), by_step(got.shape)],
        out_specs=[whole(shape) for shape, _ in shapes],
        out_shape=[jax.ShapeDtypeStruct(*shape) for shape in shapes],
        compiler_params=pltpu.CompilerParams(vmem_limit_bytes=16 * 1024 * 1024),
        cost_estimate=pl.CostEstimate(
            flops=10 * kept.size, bytes_accessed=10 * kept.size, transcendentals=0
        ),
    )(kept, got)


def body(lambda_pairs, vvvo, pair_list, owned_occ, step_root, occ_energy, virt_energy):
    window, local_b, width = vvvo.shape
    n_rows = window * local_b
    batch_pos = lax.axis_index("batch")
    slab_pos = lax.axis_index("slab")
    core = batch_pos % NC
    yh = (batch_pos // NC) % NYH
    z = batch_pos // (NC * NYH)
    x = slab_pos // NYL
    yl = slab_pos % NYL
    up = core == 0
    ahead_sign = 1 - 2 * core
    root_own = jnp.where(up, step_root[0], step_root[1])
    root_other = jnp.where(up, step_root[1], step_root[0])

    pair_list_other = send(pair_list, SWAP_CORE)

    lam = jnp.stack([lambda_pairs, send(lambda_pairs, SWAP_YL)], axis=1)
    lam = lam.reshape(2 * NYL * local_b, width)

    flat = vvvo.transpose(1, 0, 2).reshape(n_rows, width)
    far = NZ // 2

    piece = -(-n_rows // (NZ * 16)) * 16

    def ahead(sign, steps, rows=flat):
        start = jnp.minimum((z + sign * steps) % NZ * piece, n_rows - piece)
        return lax.dynamic_slice_in_dim(rows, start, piece)

    swapped = {k: send(ahead(-ahead_sign, k), SWAP_CORE) for k in (far, far - 1)}

    def inject(root, steps, theirs):
        return jnp.where(root % NC == core, ahead(ahead_sign, steps), theirs)

    def on_root(root):
        return root // NC == batch_pos // NC

    def after(array, earlier):
        return lax.optimization_barrier((array, earlier))[0]

    def both(*arrays):
        return lax.optimization_barrier(arrays)

    swapped[far], swapped[far - 1], pair_list_other = both(
        swapped[far], swapped[far - 1], pair_list_other
    )
    give_own = inject(root_own, far, swapped[far])
    flat_later = after(flat, give_own)
    for k in range(far - 2, 0, -1):
        swapped[k] = send(ahead(-ahead_sign, k, flat_later), SWAP_CORE)

    def energies(earlier):
        occ, virt, pairs, pairs_other, holds, _ = both(
            occ_energy, virt_energy, pair_list, pair_list_other, owned_occ, earlier
        )
        pairs = jnp.concatenate(
            [lax.dynamic_index_in_dim(p, core, 0) for p in (pairs, pairs_other)]
        )
        occ_sum = occ[pairs[:, 0]] + occ[pairs[:, 1]] + occ[holds[root_own]]
        energy_b = lax.dynamic_slice_in_dim(virt, slab_pos * local_b, local_b)
        energy_c = virt[:window]
        base = ((occ_sum[:, None, None] - energy_c) - energy_b[:, None]).reshape(2, n_rows)
        last = (NZ - 1) * piece
        spare = NZ * piece - n_rows
        base = jnp.concatenate(
            [base[:, :last], jnp.full((2, spare), 1e30, jnp.float32), base[:, last:]], axis=1
        ).reshape(2, NZ, piece)
        base = lax.dynamic_slice_in_dim(jnp.concatenate([base, base], axis=1), z, NZ, axis=1)
        base = jnp.where(up, jnp.roll(base[:, ::-1], 1, axis=1), base)
        ea = virt.reshape(NX, NYL, local_b)
        ea = jnp.where(yl == 0, ea, ea[:, ::-1])
        ea = lax.dynamic_slice_in_dim(jnp.concatenate([ea, ea], axis=0), x, NX, axis=0)
        ea = jnp.stack([ea, ea], axis=1).reshape(NX * 2 * NYL * local_b, 1)
        return base, ea

    got_own = send(give_own, Z_RING)
    give_other = got_other = None
    for k in range(far - 1, 0, -1):
        if give_other is not None:
            got_own = after(got_own, give_other)
        if k == far - 1:
            got_own, swapped[2], swapped[1] = both(got_own, swapped[2], swapped[1])
        elif k == far - 3:
            got_own, lam_up, lam_down = both(got_own, lam_up, lam_down)
            lam_far = [send(lam_up[: NYL * local_b], x_by(-1))]
            lam_far.append(send(lam_down[NYL * local_b :], x_by(1)))
        give_own = jnp.where(on_root(root_own), inject(root_own, k, swapped[k]), got_own)
        got_own = send(give_own, Z_RING)
        if got_other is None:
            give_other = inject(root_other, k, after(swapped[k], give_own))
            lam = after(lam, give_other)
            lam_up, lam_down = send(lam, x_by(-1)), send(lam, x_by(1))
        else:
            got_other = after(got_other, give_own)
            give_other = jnp.where(
                on_root(root_other), inject(root_other, k, swapped[k]), got_other
            )
        got_other = send(give_other, Z_RING)
    swapped[0] = send(ahead(-ahead_sign, 0, after(flat, give_other)), SWAP_CORE)
    base, ea = energies(got_own)
    got_other, _, base, ea, *lam_far = both(got_other, got_own, base, ea, *lam_far)
    crossed = send(got_other, SWAP_CORE)
    along = ((z - root_own // (NC * NYH)) * ahead_sign) % NZ
    mine = jnp.where(
        on_root(root_own),
        inject(root_own, 0, swapped[0]),
        jnp.where(along <= far, got_own, crossed),
    )
    here = jnp.where((root_own // NC) % NYH == yh, mine, send(mine, SWAP_YH))

    lams = []
    for rows in (lam, lam_up, lam_far, lam_down):
        if rows is not lam_far:
            rows = [rows[: NYL * local_b], rows[NYL * local_b :]]
        first, second = both(*rows, mine)[:2]
        got = send(jnp.where(up, second, first), SWAP_CORE)
        lams.append(jnp.concatenate([jnp.where(up, first, second), got]))

    here, *lams = both(here, *lams)
    ring_own, ring_other, crossed = [here], [send(here, SWAP_CORE)], [here]

    def base_of(order):
        return jnp.concatenate([base[:, k] for k in order], axis=1)

    total, lam = triples_call(base_of([0]), ea, lams, None, [here])
    for k in range(1, far):
        if k == 2:
            ring_own[-1], total = both(ring_own[-1], total)
        ring_own.append(send(ring_own[-1], Z_RING))
        if k == 3:
            first = [after(ring_own[1], ring_own[2]), crossed[1]]
            (total,) = triples_call(base_of([1, 7]), ea, lam, total, first)
            ring_other[-1], total = both(ring_other[-1], total)
            crossed.append(send(ring_other[-1], SWAP_CORE))
        ring_other.append(send(after(ring_other[-1], ring_own[k - 1]), Z_RING))
        if k == 1:
            crossed.append(send(ring_other[-1], SWAP_CORE))
    farthest = send(ring_own[-1], Z_RING)
    middle = [after(ring_own[2], ring_own[3]), crossed[2]]
    (total,) = triples_call(base_of([2, 6]), ea, lam, total, middle)
    late = [ring_own[3], send(after(ring_other[3], total), SWAP_CORE), farthest]
    kept, *by_x, kept_y, by_y = triples_call(base_of([3, 5, 4]), ea, lam, total, late, last=True)

    got_y = send(by_y, SWAP_YL)
    got_x = [send(by_x[step - 1], x_by(step)) for step in (2, 1, 3)]
    other, *coded = recode(kept_y, got_y)
    own = kept + sum(decode(got, width) for got in got_x)
    own = own[:local_b] + send(own[local_b:], SWAP_YL)
    got_x = [send(coded[step - 1], x_by(step)) for step in (2, 1, 3)]
    other = send(other + sum(decode(got, width) for got in got_x), SWAP_CORE)
    return jnp.where(up, jnp.stack([own, other]), jnp.stack([other, own]))


def solution(mesh):
    placed = (
        P("batch", "slab", None),
        P("batch", "slab", None),
        P("batch", None),
        P(),
        P(),
        P(),
        P(),
    )
    return jax.shard_map(
        body, mesh=mesh, in_specs=placed, out_specs=P("batch", "slab", None), check_vma=False
    )
```
